32 devices in a mesh: ctx: 8 (over y, x, core), tp: 4 (over z).
Axes of the slice: x: 2, y: 2, z: 4, core: 2. Of those that a mesh axis runs over, the one named last changes fastest.
Arguments:
- token_ids: int32 [1024], P('ctx'), may hold values from 0 to 511
- embed_table: bfloat16 [512, 8192], P(None, 'tp'), may hold values from -6 to 6
- query_feat: bfloat16 [1024, 8192], P('ctx', 'tp'), may hold values from -6 to 6
- key_feat: bfloat16 [1024, 8192], P('ctx', 'tp'), may hold values from -6 to 6
- value_feat: bfloat16 [1024, 8192], P('ctx', 'tp'), may hold values from -6 to 6
- long_filter: bfloat16 [1024, 8192], P('ctx', 'tp'), may hold values from -1.45236875 to 1.45236875
- skip_gain: float32 [8192], P('tp'), may hold values from -1 to 1
- norm_gain: bfloat16 [8192], P('tp'), may hold values from 0.099609375 to 1.8984375
- circulant_up: bfloat16 [64, 16, 512], P('tp'), may hold values from -0.0625 to 0.0625
- circulant_down: bfloat16 [16, 64, 512], P(None, 'tp'), may hold values from -0.046875 to 0.046875
Outputs:
- block_out: bfloat16 [1024, 8192], P('ctx', 'tp')
The draws below stay inside these ranges and needn't reach their ends.
All inputs are finite; a program needn't handle non-finite values.
Results may differ from the reference program's by a relative error of at most 0.01.
Values may be sent and summed in bfloat16 or wider, within the bound.
A program may use at most 128 MiB of HBM per device.

```python
import math
import jax
import jax.numpy as jnp
import numpy as np
from jax import lax

D = 8192
FF = 32768
BLOCK = 512
VOCAB = 512
TOKENS = 1024


def stream_values(key, salt):
    value_key = jax.random.fold_in(key, salt)
    values = jnp.clip(jax.random.normal(value_key, (TOKENS, D), jnp.float32), -6.0, 6.0)
    return values.astype(jnp.bfloat16)


def draw_key_feat(key, part):
    return stream_values(key, 23)


def draw_value_feat(key, part):
    return stream_values(key, 37)


def draw_long_filter(key, part):
    rate_key, value_key, tail_key, sign_key = jax.random.split(jax.random.fold_in(key, 11), 4)
    rates = jnp.exp(jax.random.uniform(rate_key, (1, D), jnp.float32, math.log(0.3), math.log(30.0)))
    position = jnp.arange(TOKENS, dtype=jnp.float32)[:, None] / TOKENS
    envelope = jnp.exp(-rates * position) * jnp.sqrt(2.0 * rates / (TOKENS * (1.0 - jnp.exp(-2.0 * rates))))
    values = jnp.clip(jax.random.normal(value_key, (TOKENS, D), jnp.float32), -6.0, 6.0)
    tail = jnp.exp(jax.random.uniform(tail_key, (1, D), jnp.float32, math.log(0.3), math.log(3.0))) / TOKENS
    signs = (2 * jax.random.randint(sign_key, (1, D), 0, 2) - 1).astype(jnp.float32)
    limit = 6.0 * math.sqrt(60.0 / TOKENS)
    return jnp.clip(values * envelope + signs * tail, -limit, limit).astype(jnp.bfloat16)


def touch_ends(entries, key, least, top_value):
    index_at = [jax.random.randint(jax.random.fold_in(key, axis), (), 0, length) for axis, length in enumerate(entries.shape)]
    main_axis = entries.shape.index(max(entries.shape))
    beside = index_at[:main_axis] + [(index_at[main_axis] + 1) % entries.shape[main_axis]] + index_at[main_axis + 1:]
    return entries.at[tuple(index_at)].set(least).at[tuple(beside)].set(top_value)


def strengthened(drawn, rng, source, target, blocks, factor):
    def block_of(axis_at):
        return (jnp.arange(drawn.shape[axis_at]) // (drawn.shape[axis_at] // blocks)).reshape((-1,) + (1,) * (drawn.ndim - 1 - axis_at))

    one_side = jax.random.permutation(rng, blocks)[block_of(target)]
    far = (block_of(target) + blocks // 2) % blocks
    return jnp.where((block_of(source) == one_side) | (block_of(source) == far), factor * drawn, drawn)


def block_scale(key, dims, shards, least, high):
    def one(dim, blocks):
        draws = jax.random.uniform(jax.random.fold_in(jax.random.fold_in(key, 6), dim), (blocks,), jnp.float32, least / len(shards), high / len(shards))
        return jnp.repeat(jnp.exp(draws), dims[dim] // blocks).reshape((-1,) + (1,) * (len(dims) - dim - 1))

    level = one(*shards[0])
    for cut in shards[1:]:
        level = level * one(*cut)
    return level


def rank_table(amount, lean):
    weights = [(1 << 20) // math.isqrt(rank ** lean) + 1 for rank in range(1, amount + 1)]
    spread = 1 + sum(weights) // (1 << 30)
    return np.cumsum(np.array([max(1, weight // spread) for weight in weights]))


def ranked_ids(key, shape, count, slope):
    listing = rank_table(count, slope)
    lot = jax.random.randint(jax.random.fold_in(key, 1), shape, 0, int(listing[count - 1]))
    grade = jnp.searchsorted(jnp.asarray(listing, jnp.int32), lot, side="right")
    return jax.random.permutation(jax.random.fold_in(key, 2), count)[grade].astype(jnp.int32)


def scatter_about(rng, extent, scale, most, pieces=(), held_as=jnp.bfloat16):
    loudness = block_scale(rng, extent, pieces, -0.22, 0.18) if pieces else 1.0
    values = jax.random.normal(rng, extent, jnp.float32) * scale * loudness
    return jnp.minimum(jnp.maximum(values, -most), most).astype(held_as)


def heavy_noise(rng, dims, spread, reach, cuts, heavy, kind=jnp.bfloat16):
    values = spread * jax.random.normal(rng, dims, jnp.float32)
    if cuts:
        values = values * block_scale(rng, dims, cuts, -0.22, 0.18)
    return jnp.clip(strengthened(values, jax.random.fold_in(rng, 3), *heavy), -reach, reach).astype(kind)


def setup_inputs(seed: int = 0) -> dict:
    seeds = jax.random.split(jax.random.key(seed), 11)
    token_ids = touch_ends(ranked_ids(seeds[0], (TOKENS,), VOCAB, 2), jax.random.fold_in(seeds[0], 3), 0, VOCAB - 1).astype(jnp.int32)
    embed_table = scatter_about(seeds[1], (VOCAB, D), 1.0, 6.0, ((1, 4),))
    query_feat = scatter_about(seeds[2], (TOKENS, D), 1.0, 6.0, ((0, 8), (1, 4)))
    key_feat = draw_key_feat(jax.random.fold_in(seeds[10], 71), 0)
    value_feat = draw_value_feat(jax.random.fold_in(seeds[10], 71), 0)
    long_filter = draw_long_filter(jax.random.fold_in(seeds[10], 71), 0)
    skip_gain = jnp.clip(jax.random.uniform(seeds[6], (D,), jnp.float32, -1.0, 1.0) * block_scale(seeds[6], (D,), ((0, 4),), -0.4, 0.0), -1.0, 1.0)
    norm_gain = jnp.clip(1.0 + 0.18 * jax.random.normal(seeds[7], (D,), jnp.float32), 0.099609375, 1.8984375).astype(jnp.bfloat16)
    circulant_up = scatter_about(seeds[8], (FF // BLOCK, D // BLOCK, BLOCK), D ** -0.5, 0.0625, ((0, 4),))
    circulant_down = heavy_noise(seeds[9], (D // BLOCK, FF // BLOCK, BLOCK), FF ** -0.5, 0.046875, ((1, 4),), (1, 0, 4, 2.0))
    return dict(token_ids=token_ids, embed_table=embed_table, query_feat=query_feat, key_feat=key_feat, value_feat=value_feat, long_filter=long_filter, skip_gain=skip_gain, norm_gain=norm_gain, circulant_up=circulant_up, circulant_down=circulant_down)


def causal_mix(gated, taps):
    length = gated.shape[0]
    width = gated.shape[1]
    group = min(512, width)
    count = width // group

    def one_group(arrays):
        signal, kernel = arrays
        spec_signal = jnp.fft.rfft(signal, n=2 * length, axis=0)
        spec_kernel = jnp.fft.rfft(kernel, n=2 * length, axis=0)
        return jnp.fft.irfft(spec_signal * spec_kernel, n=2 * length, axis=0)[:length]
    signal_groups = gated.astype(jnp.float32).reshape(length, count, group).transpose(1, 0, 2)
    kernel_groups = taps.astype(jnp.float32).reshape(length, count, group).transpose(1, 0, 2)
    mixed = lax.map(one_group, (signal_groups, kernel_groups))
    return mixed.transpose(1, 0, 2).reshape(length, width)

def circulant_apply(inputs, weights):
    count = inputs.shape[0]
    spec_weights = jnp.fft.rfft(weights.astype(jnp.float32), axis=2)
    group = min(256, count)

    def one_group(block_rows):
        spec_rows = jnp.fft.rfft(block_rows.astype(jnp.float32).reshape(group, -1, BLOCK), axis=2)
        spec_out = jnp.einsum('tjf,ijf->tif', spec_rows, spec_weights)
        return jnp.fft.irfft(spec_out, n=BLOCK, axis=2).reshape(group, -1)
    result = lax.map(one_group, inputs.reshape(count // group, group, -1))
    return result.reshape(count, -1)

def reference(token_ids, embed_table, query_feat, key_feat, value_feat, long_filter, skip_gain, norm_gain, circulant_up, circulant_down):
    embedded = embed_table[token_ids].astype(jnp.float32)
    gated = (key_feat.astype(jnp.float32) * value_feat.astype(jnp.float32)).astype(jnp.bfloat16)
    gated_wide = gated.astype(jnp.float32)
    mixed = causal_mix(gated, long_filter) + skip_gain[None, :] * gated_wide
    stream = (embedded + query_feat.astype(jnp.float32) * mixed).astype(jnp.bfloat16)
    stream_wide = stream.astype(jnp.float32)
    scale_row = lax.rsqrt(lax.optimization_barrier(jnp.mean(stream_wide * stream_wide, axis=1, keepdims=True)) + 1e-06)
    normed = (stream_wide * scale_row * norm_gain.astype(jnp.float32)[None, :]).astype(jnp.bfloat16)
    hidden_pre = circulant_apply(normed, circulant_up)
    hidden = jax.nn.gelu(hidden_pre, approximate=False).astype(jnp.bfloat16)
    branch = circulant_apply(hidden, circulant_down)
    return (stream_wide + branch).astype(jnp.bfloat16)
```

```python
import functools
import math

import jax
import jax.numpy as jnp
import numpy as np
from jax import lax
from jax.experimental import pallas as pl
from jax.experimental.pallas import tpu as pltpu
from jax.sharding import PartitionSpec as P

D = 8192
BLOCK = 512
HALF = BLOCK // 2
LANES = 128
DENSE_WINDOW = 2048


precise = lax.Precision.HIGHEST
full_turn = 6.283185307179586


def angles(first, second, period, offset):
    left_index = lax.broadcasted_iota(jnp.int32, (first, second), 0)
    right_index = lax.broadcasted_iota(jnp.int32, (first, second), 1) + offset
    return full_turn / period * (left_index * right_index % period).astype(jnp.float32)


def placed(table, layout):
    shape = []
    for letter in layout:
        if letter == "k":
            shape.append(table.shape[0])
        elif letter == "m":
            shape.append(table.shape[1])
        else:
            shape.append(1)
    return table.reshape(shape)


def contract(layout, values, table, source, target):
    result = layout.replace(source, target)
    return jnp.einsum(
        layout + "," + source + target + "->" + result, values, table, precision=precise
    )


def forward_outer(values, layout, offset, period):
    outer = values.shape[layout.index("p")]
    inner = values.shape[layout.index("m")]
    table = angles(outer, 2 * outer, 2 * outer, 0)
    widened = values.astype(jnp.float32)
    real_part = contract(layout, widened, jnp.cos(table), "p", "k")
    imag_part = -contract(layout, widened, jnp.sin(table), "p", "k")
    turned = layout.replace("p", "k")
    twist = angles(2 * outer, inner, period, offset)
    cosine = placed(jnp.cos(twist), turned)
    sine = placed(jnp.sin(twist), turned)
    return (real_part * cosine + imag_part * sine, imag_part * cosine - real_part * sine)


def forward_inner(real_part, imag_part, layout):
    inner = real_part.shape[layout.index("m")]
    table = angles(inner, inner, inner, 0)
    cosine = jnp.cos(table)
    sine = jnp.sin(table)
    new_real = contract(layout, real_part, cosine, "m", "n") + contract(
        layout, imag_part, sine, "m", "n"
    )
    new_imag = contract(layout, imag_part, cosine, "m", "n") - contract(
        layout, real_part, sine, "m", "n"
    )
    return (new_real, new_imag)


def inverse_inner(real_part, imag_part, layout):
    inner = real_part.shape[layout.index("m")]
    table = angles(inner, inner, inner, 0)
    cosine = jnp.cos(table)
    sine = jnp.sin(table)
    new_real = contract(layout, real_part, cosine, "m", "n") - contract(
        layout, imag_part, sine, "m", "n"
    )
    new_imag = contract(layout, imag_part, cosine, "m", "n") + contract(
        layout, real_part, sine, "m", "n"
    )
    return (new_real, new_imag)


def inverse_outer(real_part, imag_part, layout, offset, period):
    doubled = real_part.shape[layout.index("k")]
    inner = real_part.shape[layout.index("m")]
    twist = angles(doubled, inner, period, offset)
    cosine = placed(jnp.cos(twist), layout)
    sine = placed(jnp.sin(twist), layout)
    turned_real = real_part * cosine - imag_part * sine
    turned_imag = imag_part * cosine + real_part * sine
    table = angles(doubled, doubled // 2, doubled, 0)
    summed = contract(layout, turned_real, jnp.cos(table), "k", "p") - contract(
        layout, turned_imag, jnp.sin(table), "k", "p"
    )
    return summed / period


def spectral_product(real_part, imag_part):
    real_out = real_part[0] * real_part[1] - imag_part[0] * imag_part[1]
    imag_out = real_part[0] * imag_part[1] + imag_part[0] * real_part[1]
    return (real_out, imag_out)


def packed_dft(size, rows):
    half = size // 2
    turn = (np.arange(rows)[:, None] * np.arange(half)[None, :]) % size
    angle = 2.0 * np.pi / size * turn
    cosine = np.cos(angle)
    sine = -np.sin(angle)
    sine[:, 0] = 1.0 - 2.0 * (np.arange(rows) % 2)
    return cosine, sine


def packed_weights(size):
    half = size // 2
    weight = np.full((half,), 2.0 / size)
    weight[0] = 1.0 / size
    return weight


def block_tables():
    cosine, sine = packed_dft(BLOCK, BLOCK)
    forward = np.concatenate([cosine, sine], axis=1)
    weight = packed_weights(BLOCK)
    inverse = np.concatenate([cosine * weight, sine * weight], axis=1).T
    cross = sine.copy()
    cross[:, 0] = 0.0
    straight = cosine.copy()
    straight[:, 0] = sine[:, 0]
    taps = np.concatenate([cross, cosine + cross, straight - cross], axis=1)
    return (
        jnp.asarray(forward, jnp.bfloat16),
        jnp.asarray(inverse, jnp.bfloat16),
        jnp.asarray(taps, jnp.bfloat16),
    )


def short_window(signal, kernel):
    length, width = signal.shape
    cosine, sine = packed_dft(2 * length, length)
    table = jnp.asarray(np.concatenate([cosine, sine], axis=1).T, jnp.bfloat16)
    both = jnp.concatenate([signal, kernel], axis=1)
    spectrum = jnp.dot(table, both, preferred_element_type=jnp.float32)
    real_s, real_k = spectrum[:length, :width], spectrum[:length, width:]
    imag_s, imag_k = spectrum[length:, :width], spectrum[length:, width:]
    first = lax.broadcasted_iota(jnp.int32, (length, 1), 0) == 0
    weight = jnp.asarray(packed_weights(2 * length)[:, None], jnp.float32)
    crossed = imag_s * imag_k
    real_out = weight * (real_s * real_k - jnp.where(first, 0.0, crossed))
    imag_out = weight * jnp.where(first, crossed, real_s * imag_k + imag_s * real_k)
    product = jnp.concatenate([real_out, imag_out], axis=0).astype(jnp.bfloat16)
    return lax.dot_general(
        table, product, (((0,), (0,)), ((), ())), preferred_element_type=jnp.float32
    )


def long_window(signal, kernel, outer):
    period = 2 * signal.shape[0]
    tokens = signal.shape[0] // outer
    stacked = jnp.stack([signal, kernel]).reshape(2, outer, tokens, -1).transpose(0, 3, 1, 2)
    real_part, imag_part = forward_outer(stacked, "scpm", 0, period)
    real_part, imag_part = forward_inner(real_part, imag_part, "sckm")
    real_part, imag_part = spectral_product(real_part, imag_part)
    real_part, imag_part = inverse_inner(real_part, imag_part, "ckm")
    local_mixed = inverse_outer(real_part, imag_part, "ckm", 0, period)
    return local_mixed.transpose(1, 2, 0).reshape(outer * tokens, -1)


def mix_blocks(tokens, outs, ins, chunk, real_ref, imag_ref, sum_ref, w_ref, spec_ref, row_of):
    for half in range(HALF // LANES):
        lanes = pl.ds(half * LANES, LANES)

        @pl.loop(0, outs // 2)
        def _(pair):
            def step(part, totals):
                totals = list(totals)
                for inner in range(chunk):
                    if inner % 8 == 0:
                        held = [
                            [
                                w_ref[
                                    pl.ds(pl.multiple_of(row_of(pair * 2 + b, part, inner), 8), 8),
                                    k * HALF + half * LANES : k * HALF + (half + 1) * LANES,
                                ]
                                for k in range(3)
                            ]
                            for b in range(2)
                        ]
                    rows = pl.ds(pl.multiple_of((part * chunk + inner) * tokens, tokens), tokens)
                    real = real_ref[rows, lanes]
                    imag = imag_ref[rows, lanes]
                    both = sum_ref[rows, lanes]
                    at = inner % 8
                    for b in range(2):
                        w0, w1, w2 = [held[b][k][at : at + 1] for k in range(3)]
                        totals[3 * b] = totals[3 * b] + w0 * both
                        totals[3 * b + 1] = totals[3 * b + 1] + w1 * real
                        totals[3 * b + 2] = totals[3 * b + 2] + w2 * imag
                return tuple(totals)

            zero = jnp.zeros((tokens, LANES), jnp.float32)
            totals = (zero,) * 6
            if ins == chunk:
                totals = step(0, totals)
            else:
                totals = lax.fori_loop(0, ins // chunk, step, totals)
            for b in range(2):
                rows = pl.ds(pl.multiple_of((pair * 2 + b) * tokens, tokens), tokens)
                cross, real, imag = totals[3 * b : 3 * b + 3]
                spec_ref[rows, half * LANES : (half + 1) * LANES] = (real - cross).astype(
                    jnp.bfloat16
                )
                spec_ref[rows, HALF + half * LANES : HALF + (half + 1) * LANES] = (
                    cross + imag
                ).astype(jnp.bfloat16)


def mlp_kernel(
    tiles,
    x_ref,
    gain_ref,
    w_ref,
    fwd_ref,
    inv_ref,
    out_ref,
    rows_ref,
    hid_ref,
    spec_ref,
    real_ref,
    imag_ref,
    sum_ref,
):
    groups, tokens, width = x_ref.shape
    per_group = width // BLOCK
    ins = groups * per_group
    stride = w_ref.shape[0] // groups
    local = tiles // groups
    squares = jnp.zeros((tokens, 1), jnp.float32)
    for p in range(groups):
        wide = x_ref[p].astype(jnp.float32)
        squares = squares + jnp.sum(wide * wide, axis=1, keepdims=True)
    scale = lax.rsqrt(squares / (groups * width) + 1e-06)
    for j in range(ins):
        p, at = j // per_group, (j % per_group) * BLOCK
        wide = x_ref[p, :, at : at + BLOCK].astype(jnp.float32)
        gain = gain_ref[j : j + 1, :].astype(jnp.float32)
        rows_ref[j * tokens : (j + 1) * tokens, :] = (wide * scale * gain).astype(jnp.bfloat16)

    piece = 256

    def forward(values_ref, total):
        @pl.loop(0, total // piece)
        def _(at):
            rows = pl.ds(pl.multiple_of(at * piece, piece), piece)
            spec = jnp.dot(values_ref[rows, :], fwd_ref[...], preferred_element_type=jnp.float32)
            real_ref[rows, :] = spec[:, :HALF]
            imag_ref[rows, :] = spec[:, HALF:]
            sum_ref[rows, :] = spec[:, :HALF] + spec[:, HALF:]

    forward(rows_ref, ins * tokens)

    def up_row(i, part, inner):
        return (i // local) * stride + (i % local) * ins + inner

    mix_blocks(tokens, tiles, ins, ins, real_ref, imag_ref, sum_ref, w_ref, spec_ref, up_row)

    @pl.loop(0, tiles * tokens // piece)
    def _(at):
        rows = pl.ds(pl.multiple_of(at * piece, piece), piece)
        pre = jnp.dot(spec_ref[rows, :], inv_ref[...], preferred_element_type=jnp.float32)
        hidden = 0.5 * pre * (1.0 + lax.erf(pre * math.sqrt(0.5)))
        hid_ref[rows, :] = hidden.astype(jnp.bfloat16)

    forward(hid_ref, tiles * tokens)

    def down_row(i, part, inner):
        return part * stride + local * ins + i * local + inner

    mix_blocks(tokens, ins, tiles, local, real_ref, imag_ref, sum_ref, w_ref, spec_ref, down_row)
    for i in range(ins):
        p, at = i // per_group, (i % per_group) * BLOCK
        branch = jnp.dot(
            spec_ref[i * tokens : (i + 1) * tokens, :],
            inv_ref[...],
            preferred_element_type=jnp.float32,
        )
        wide = x_ref[p, :, at : at + BLOCK].astype(jnp.float32)
        out_ref[p, :, at : at + BLOCK] = (wide + branch).astype(jnp.bfloat16)


def mlp(stream, gain, taps, tiles, forward_table, inverse_table):
    groups, tokens, width = stream.shape
    total = tiles * tokens
    wide = pltpu.VMEM((total, HALF), jnp.float32)
    return pl.pallas_call(
        functools.partial(mlp_kernel, tiles),
        out_shape=jax.ShapeDtypeStruct(stream.shape, jnp.bfloat16),
        in_specs=[pl.BlockSpec(memory_space=pltpu.VMEM)] * 5,
        out_specs=pl.BlockSpec(memory_space=pltpu.VMEM),
        scratch_shapes=[
            pltpu.VMEM((groups * width // BLOCK * tokens, BLOCK), jnp.bfloat16),
            pltpu.VMEM((total, BLOCK), jnp.bfloat16),
            pltpu.VMEM((total, BLOCK), jnp.bfloat16),
            wide,
            wide,
            wide,
        ],
        compiler_params=pltpu.CompilerParams(vmem_limit_bytes=40 * 1024 * 1024),
        name="circulant_mlp",
    )(stream, gain, taps, forward_table, inverse_table)


def body(
    token_ids,
    embed_table,
    query_feat,
    key_feat,
    value_feat,
    long_filter,
    skip_gain,
    norm_gain,
    circulant_up,
    circulant_down,
):
    tokens = token_ids.shape[0]
    vocab = embed_table.shape[0]
    outer = lax.axis_size("ctx")
    groups = lax.axis_size("tp")
    width = query_feat.shape[1]
    ins = circulant_up.shape[1]
    local = circulant_up.shape[0]
    gated_wide = key_feat.astype(jnp.float32) * value_feat.astype(jnp.float32)
    gated = gated_wide.astype(jnp.bfloat16)
    arrived_signal, arrived_kernel = (
        lax.all_to_all(gated, "ctx", split_axis=1, concat_axis=0, tiled=True),
        lax.all_to_all(long_filter, "ctx", split_axis=1, concat_axis=0, tiled=True),
    )
    forward_table, inverse_table, tap_table = block_tables()
    gain_rows = norm_gain.reshape(-1, BLOCK)
    padded = 16
    gain_rows = jnp.pad(gain_rows, ((0, padded - gain_rows.shape[0]), (0, 0)))
    columns = jnp.concatenate(
        [circulant_up.reshape(-1, BLOCK), circulant_down.reshape(-1, BLOCK), gain_rows], axis=0
    )
    all_columns = lax.all_gather(columns, "tp", axis=0, tiled=True)
    taps = jnp.dot(all_columns, tap_table, preferred_element_type=jnp.float32)
    full_gain = all_columns.reshape(groups, -1, BLOCK)[:, -padded : width // BLOCK - padded, :]
    full_gain = full_gain.reshape(-1, BLOCK)
    onehot = (token_ids[:, None] == lax.broadcasted_iota(jnp.int32, (1, vocab), 1)).astype(
        jnp.bfloat16
    )
    embedded = jnp.dot(onehot, embed_table, preferred_element_type=jnp.float32)
    if outer * tokens <= DENSE_WINDOW:
        local_mixed = short_window(arrived_signal, arrived_kernel)
    else:
        local_mixed = long_window(arrived_signal, arrived_kernel, outer)
    mixed = lax.all_to_all(
        local_mixed.astype(jnp.bfloat16), "ctx", split_axis=0, concat_axis=1, tiled=True
    ).astype(jnp.float32)
    mixed = mixed + skip_gain[None, :] * gated.astype(jnp.float32)
    stream = (embedded + query_feat.astype(jnp.float32) * mixed).astype(jnp.bfloat16)
    own = lax.all_to_all(
        stream.reshape(groups, tokens // groups, width), "tp", split_axis=0, concat_axis=0
    )
    result = mlp(own, full_gain, taps, local * groups, forward_table, inverse_table)
    return lax.all_to_all(result, "tp", split_axis=0, concat_axis=0).reshape(tokens, width)


def solution(mesh):
    placed = (
        P("ctx"),
        P(None, "tp"),
        P("ctx", "tp"),
        P("ctx", "tp"),
        P("ctx", "tp"),
        P("ctx", "tp"),
        P("tp"),
        P("tp"),
        P("tp", None, None),
        P(None, "tp", None),
    )
    return jax.shard_map(
        body, mesh=mesh, in_specs=placed, out_specs=P("ctx", "tp"), check_vma=False
    )
```

```python
import functools
import math

import jax
import jax.numpy as jnp
import numpy as np
from jax import lax
from jax.experimental import pallas as pl
from jax.experimental.pallas import tpu as pltpu
from jax.sharding import PartitionSpec as P

D = 8192
BLOCK = 512
HALF = BLOCK // 2
LANES = 128
DENSE_WINDOW = 2048


precise = lax.Precision.HIGHEST
full_turn = 6.283185307179586


def angles(first, second, period, offset):
    left_index = lax.broadcasted_iota(jnp.int32, (first, second), 0)
    right_index = lax.broadcasted_iota(jnp.int32, (first, second), 1) + offset
    return full_turn / period * (left_index * right_index % period).astype(jnp.float32)


def placed(table, layout):
    shape = []
    for letter in layout:
        if letter == "k":
            shape.append(table.shape[0])
        elif letter == "m":
            shape.append(table.shape[1])
        else:
            shape.append(1)
    return table.reshape(shape)


def contract(layout, values, table, source, target):
    result = layout.replace(source, target)
    return jnp.einsum(
        layout + "," + source + target + "->" + result, values, table, precision=precise
    )


def forward_outer(values, layout, offset, period):
    outer = values.shape[layout.index("p")]
    inner = values.shape[layout.index("m")]
    table = angles(outer, 2 * outer, 2 * outer, 0)
    widened = values.astype(jnp.float32)
    real_part = contract(layout, widened, jnp.cos(table), "p", "k")
    imag_part = -contract(layout, widened, jnp.sin(table), "p", "k")
    turned = layout.replace("p", "k")
    twist = angles(2 * outer, inner, period, offset)
    cosine = placed(jnp.cos(twist), turned)
    sine = placed(jnp.sin(twist), turned)
    return (real_part * cosine + imag_part * sine, imag_part * cosine - real_part * sine)


def forward_inner(real_part, imag_part, layout):
    inner = real_part.shape[layout.index("m")]
    table = angles(inner, inner, inner, 0)
    cosine = jnp.cos(table)
    sine = jnp.sin(table)
    new_real = contract(layout, real_part, cosine, "m", "n") + contract(
        layout, imag_part, sine, "m", "n"
    )
    new_imag = contract(layout, imag_part, cosine, "m", "n") - contract(
        layout, real_part, sine, "m", "n"
    )
    return (new_real, new_imag)


def inverse_inner(real_part, imag_part, layout):
    inner = real_part.shape[layout.index("m")]
    table = angles(inner, inner, inner, 0)
    cosine = jnp.cos(table)
    sine = jnp.sin(table)
    new_real = contract(layout, real_part, cosine, "m", "n") - contract(
        layout, imag_part, sine, "m", "n"
    )
    new_imag = contract(layout, imag_part, cosine, "m", "n") + contract(
        layout, real_part, sine, "m", "n"
    )
    return (new_real, new_imag)


def inverse_outer(real_part, imag_part, layout, offset, period):
    doubled = real_part.shape[layout.index("k")]
    inner = real_part.shape[layout.index("m")]
    twist = angles(doubled, inner, period, offset)
    cosine = placed(jnp.cos(twist), layout)
    sine = placed(jnp.sin(twist), layout)
    turned_real = real_part * cosine - imag_part * sine
    turned_imag = imag_part * cosine + real_part * sine
    table = angles(doubled, doubled // 2, doubled, 0)
    summed = contract(layout, turned_real, jnp.cos(table), "k", "p") - contract(
        layout, turned_imag, jnp.sin(table), "k", "p"
    )
    return summed / period


def spectral_product(real_part, imag_part):
    real_out = real_part[0] * real_part[1] - imag_part[0] * imag_part[1]
    imag_out = real_part[0] * imag_part[1] + imag_part[0] * real_part[1]
    return (real_out, imag_out)


def packed_dft(size, rows):
    half = size // 2
    turn = (np.arange(rows)[:, None] * np.arange(half)[None, :]) % size
    angle = 2.0 * np.pi / size * turn
    cosine = np.cos(angle)
    sine = -np.sin(angle)
    sine[:, 0] = 1.0 - 2.0 * (np.arange(rows) % 2)
    return cosine, sine


def packed_weights(size):
    half = size // 2
    weight = np.full((half,), 2.0 / size)
    weight[0] = 1.0 / size
    return weight


def block_tables():
    cosine, sine = packed_dft(BLOCK, BLOCK)
    forward = np.concatenate([cosine, sine], axis=1)
    weight = packed_weights(BLOCK)
    inverse = np.concatenate([cosine * weight, sine * weight], axis=1).T
    cross = sine.copy()
    cross[:, 0] = 0.0
    straight = cosine.copy()
    straight[:, 0] = sine[:, 0]
    taps = np.concatenate([cross, cosine + cross, straight - cross], axis=1)
    return (
        jnp.asarray(forward, jnp.bfloat16),
        jnp.asarray(inverse, jnp.bfloat16),
        jnp.asarray(taps, jnp.bfloat16),
    )


def short_window(both):
    length, width = both.shape[0], both.shape[1] // 2
    cosine, sine = packed_dft(2 * length, length)
    table = jnp.asarray(np.concatenate([cosine, sine], axis=1).T, jnp.bfloat16)
    spectrum = jnp.dot(table, both, preferred_element_type=jnp.float32)
    real_s, real_k = spectrum[:length, :width], spectrum[:length, width:]
    imag_s, imag_k = spectrum[length:, :width], spectrum[length:, width:]
    first = lax.broadcasted_iota(jnp.int32, (length, 1), 0) == 0
    weight = jnp.asarray(packed_weights(2 * length)[:, None], jnp.float32)
    crossed = imag_s * imag_k
    real_out = weight * (real_s * real_k - jnp.where(first, 0.0, crossed))
    imag_out = weight * jnp.where(first, crossed, real_s * imag_k + imag_s * real_k)
    product = jnp.concatenate([real_out, imag_out], axis=0).astype(jnp.bfloat16)
    return lax.dot_general(
        table, product, (((0,), (0,)), ((), ())), preferred_element_type=jnp.float32
    )


def long_window(signal, kernel, outer):
    period = 2 * signal.shape[0]
    tokens = signal.shape[0] // outer
    stacked = jnp.stack([signal, kernel]).reshape(2, outer, tokens, -1).transpose(0, 3, 1, 2)
    real_part, imag_part = forward_outer(stacked, "scpm", 0, period)
    real_part, imag_part = forward_inner(real_part, imag_part, "sckm")
    real_part, imag_part = spectral_product(real_part, imag_part)
    real_part, imag_part = inverse_inner(real_part, imag_part, "ckm")
    local_mixed = inverse_outer(real_part, imag_part, "ckm", 0, period)
    return local_mixed.transpose(1, 2, 0).reshape(outer * tokens, -1)


def mix_blocks(tokens, outs, ins, chunk, real_ref, imag_ref, sum_ref, w_ref, spec_ref, row_of):
    for half in range(HALF // LANES):
        lanes = pl.ds(half * LANES, LANES)

        @pl.loop(0, outs // 2)
        def _(pair):
            def step(part, totals):
                totals = list(totals)
                for inner in range(chunk):
                    if inner % 8 == 0:
                        held = [
                            [
                                w_ref[
                                    pl.ds(pl.multiple_of(row_of(pair * 2 + b, part, inner), 8), 8),
                                    k * HALF + half * LANES : k * HALF + (half + 1) * LANES,
                                ]
                                for k in range(3)
                            ]
                            for b in range(2)
                        ]
                    rows = pl.ds(pl.multiple_of((part * chunk + inner) * tokens, tokens), tokens)
                    real = real_ref[rows, lanes]
                    imag = imag_ref[rows, lanes]
                    both = sum_ref[rows, lanes]
                    at = inner % 8
                    for b in range(2):
                        w0, w1, w2 = [held[b][k][at : at + 1] for k in range(3)]
                        totals[3 * b] = totals[3 * b] + w0 * both
                        totals[3 * b + 1] = totals[3 * b + 1] + w1 * real
                        totals[3 * b + 2] = totals[3 * b + 2] + w2 * imag
                return tuple(totals)

            zero = jnp.zeros((tokens, LANES), jnp.float32)
            totals = (zero,) * 6
            if ins == chunk:
                totals = step(0, totals)
            else:
                totals = lax.fori_loop(0, ins // chunk, step, totals)
            for b in range(2):
                rows = pl.ds(pl.multiple_of((pair * 2 + b) * tokens, tokens), tokens)
                cross, real, imag = totals[3 * b : 3 * b + 3]
                spec_ref[rows, half * LANES : (half + 1) * LANES] = (real - cross).astype(
                    jnp.bfloat16
                )
                spec_ref[rows, HALF + half * LANES : HALF + (half + 1) * LANES] = (
                    cross + imag
                ).astype(jnp.bfloat16)


def mlp_kernel(
    local,
    mine_ref,
    cols_ref,
    fwd_ref,
    inv_ref,
    tap_ref,
    out_ref,
    x_ref,
    done_ref,
    w_ref,
    rows_ref,
    hid_ref,
    spec_ref,
    real_ref,
    imag_ref,
    sum_ref,
    send_sem,
    recv_sem,
    back_send_sem,
    back_recv_sem,
):
    groups, tokens, width = mine_ref.shape
    per_group = width // BLOCK
    ins = groups * per_group
    tiles = groups * local
    stride = 2 * local * ins
    held = cols_ref.shape[0] // groups
    me = lax.axis_index("tp")
    peers = [lax.rem(me + d, groups) for d in range(1, groups)]

    barrier = pltpu.get_barrier_semaphore()
    for peer in peers:
        pl.semaphore_signal(
            barrier, inc=1, device_id={"tp": peer}, device_id_type=pl.DeviceIdType.MESH
        )
    pl.semaphore_wait(barrier, groups - 1)

    def send(d, src, dst, sent, got):
        copy = pltpu.make_async_remote_copy(
            src_ref=src.at[peers[d]],
            dst_ref=dst.at[me],
            send_sem=sent.at[d],
            recv_sem=got.at[d],
            device_id={"tp": peers[d]},
            device_id_type=pl.DeviceIdType.MESH,
        )
        copy.start()
        return copy

    copies = [send(d, mine_ref, x_ref, send_sem, recv_sem) for d in range(groups - 1)]
    x_ref[me] = mine_ref[me]
    for p in range(groups):
        for part in range(2):
            at = part * local * ins
            w_ref[p * stride + at : p * stride + at + local * ins, :] = jnp.dot(
                cols_ref[p * held + at : p * held + at + local * ins, :],
                tap_ref[...],
                preferred_element_type=jnp.float32,
            )
    for copy in copies:
        copy.wait()

    squares = jnp.zeros((tokens, 1), jnp.float32)
    for p in range(groups):
        wide = x_ref[p].astype(jnp.float32)
        squares = squares + jnp.sum(wide * wide, axis=1, keepdims=True)
    scale = lax.rsqrt(squares / (groups * width) + 1e-06)
    for j in range(ins):
        p, at = j // per_group, (j % per_group) * BLOCK
        wide = x_ref[p, :, at : at + BLOCK].astype(jnp.float32)
        row = p * held + stride + j % per_group
        gain = cols_ref[row : row + 1, :].astype(jnp.float32)
        rows_ref[j * tokens : (j + 1) * tokens, :] = (wide * scale * gain).astype(jnp.bfloat16)

    piece = 256

    def forward(values_ref, total):
        @pl.loop(0, total // piece)
        def _(at):
            rows = pl.ds(pl.multiple_of(at * piece, piece), piece)
            spec = jnp.dot(values_ref[rows, :], fwd_ref[...], preferred_element_type=jnp.float32)
            real_ref[rows, :] = spec[:, :HALF]
            imag_ref[rows, :] = spec[:, HALF:]
            sum_ref[rows, :] = spec[:, :HALF] + spec[:, HALF:]

    forward(rows_ref, ins * tokens)

    def up_row(i, part, inner):
        return (i // local) * stride + (i % local) * ins + inner

    mix_blocks(tokens, tiles, ins, ins, real_ref, imag_ref, sum_ref, w_ref, spec_ref, up_row)

    @pl.loop(0, tiles * tokens // piece)
    def _(at):
        rows = pl.ds(pl.multiple_of(at * piece, piece), piece)
        pre = jnp.dot(spec_ref[rows, :], inv_ref[...], preferred_element_type=jnp.float32)
        hidden = 0.5 * pre * (1.0 + lax.erf(pre * math.sqrt(0.5)))
        hid_ref[rows, :] = hidden.astype(jnp.bfloat16)

    forward(hid_ref, tiles * tokens)

    copies = []
    for d in range(groups):
        target = peers[d] if d < groups - 1 else me

        def down_row(i, part, inner):
            return part * stride + local * ins + (target * per_group + i) * local + inner

        mix_blocks(
            tokens, per_group, tiles, local, real_ref, imag_ref, sum_ref, w_ref, spec_ref, down_row
        )
        branch = jnp.dot(
            spec_ref[: per_group * tokens, :], inv_ref[...], preferred_element_type=jnp.float32
        )
        for i in range(per_group):
            at = i * BLOCK
            wide = x_ref[target, :, at : at + BLOCK].astype(jnp.float32)
            total = (wide + branch[i * tokens : (i + 1) * tokens]).astype(jnp.bfloat16)
            if d < groups - 1:
                done_ref[target, :, at : at + BLOCK] = total
            else:
                out_ref[target, :, at : at + BLOCK] = total
        if d < groups - 1:
            copies.append(send(d, done_ref, out_ref, back_send_sem, back_recv_sem))
    for copy in copies:
        copy.wait()


def mlp(stream, columns, local, forward_table, inverse_table, tap_table):
    groups, tokens, width = stream.shape
    ins = groups * width // BLOCK
    total = groups * local * tokens
    wide = pltpu.VMEM((total, HALF), jnp.float32)
    arrivals = pltpu.SemaphoreType.DMA((groups - 1,))
    return pl.pallas_call(
        functools.partial(mlp_kernel, local),
        out_shape=jax.ShapeDtypeStruct(stream.shape, jnp.bfloat16),
        in_specs=[pl.BlockSpec(memory_space=pltpu.VMEM)] * 5,
        out_specs=pl.BlockSpec(memory_space=pltpu.VMEM),
        scratch_shapes=[
            pltpu.VMEM(stream.shape, jnp.bfloat16),
            pltpu.VMEM(stream.shape, jnp.bfloat16),
            pltpu.VMEM((2 * groups * local * ins, 3 * HALF), jnp.float32),
            pltpu.VMEM((ins * tokens, BLOCK), jnp.bfloat16),
            pltpu.VMEM((total, BLOCK), jnp.bfloat16),
            pltpu.VMEM((total, BLOCK), jnp.bfloat16),
            wide,
            wide,
            wide,
            arrivals,
            arrivals,
            arrivals,
            arrivals,
        ],
        compiler_params=pltpu.CompilerParams(
            vmem_limit_bytes=40 * 1024 * 1024, collective_id=1, has_side_effects=True
        ),
        name="circulant_mlp",
    )(stream, columns, forward_table, inverse_table, tap_table)


def body(
    token_ids,
    embed_table,
    query_feat,
    key_feat,
    value_feat,
    long_filter,
    skip_gain,
    norm_gain,
    circulant_up,
    circulant_down,
):
    tokens = token_ids.shape[0]
    vocab = embed_table.shape[0]
    outer = lax.axis_size("ctx")
    groups = lax.axis_size("tp")
    width = query_feat.shape[1]
    ins = circulant_up.shape[1]
    local = circulant_up.shape[0]
    gated_wide = key_feat.astype(jnp.float32) * value_feat.astype(jnp.float32)
    gated = gated_wide.astype(jnp.bfloat16)
    pairs = jnp.concatenate(
        [gated.reshape(tokens, outer, -1), long_filter.reshape(tokens, outer, -1)], axis=2
    )
    arrived = lax.all_to_all(pairs, "ctx", split_axis=1, concat_axis=0)
    arrived = arrived.reshape(outer * tokens, -1)
    forward_table, inverse_table, tap_table = block_tables()
    gain_rows = norm_gain.reshape(-1, BLOCK)
    padded = 16
    gain_rows = jnp.pad(gain_rows, ((0, padded - gain_rows.shape[0]), (0, 0)))
    columns = jnp.concatenate(
        [circulant_up.reshape(-1, BLOCK), circulant_down.reshape(-1, BLOCK), gain_rows], axis=0
    )
    all_columns = lax.all_gather(columns, "tp", axis=0, tiled=True)
    onehot = (token_ids[:, None] == lax.broadcasted_iota(jnp.int32, (1, vocab), 1)).astype(
        jnp.bfloat16
    )
    embedded = jnp.dot(onehot, embed_table, preferred_element_type=jnp.float32)
    if outer * tokens <= DENSE_WINDOW:
        local_mixed = short_window(arrived)
    else:
        local_mixed = long_window(*jnp.split(arrived, 2, axis=1), outer)
    mixed = lax.all_to_all(
        local_mixed.astype(jnp.bfloat16), "ctx", split_axis=0, concat_axis=1, tiled=True
    ).astype(jnp.float32)
    mixed = mixed + skip_gain[None, :] * gated.astype(jnp.float32)
    stream = (embedded + query_feat.astype(jnp.float32) * mixed).astype(jnp.bfloat16)
    own = stream.reshape(groups, tokens // groups, width)
    result = mlp(own, all_columns, local, forward_table, inverse_table, tap_table)
    return result.reshape(tokens, width)


def solution(mesh):
    placed = (
        P("ctx"),
        P(None, "tp"),
        P("ctx", "tp"),
        P("ctx", "tp"),
        P("ctx", "tp"),
        P("ctx", "tp"),
        P("tp"),
        P("tp"),
        P("tp", None, None),
        P(None, "tp", None),
    )
    return jax.shard_map(
        body, mesh=mesh, in_specs=placed, out_specs=P("ctx", "tp"), check_vma=False
    )
```

```python
import functools
import math

import jax
import jax.numpy as jnp
import numpy as np
from jax import lax
from jax.experimental import pallas as pl
from jax.experimental.pallas import tpu as pltpu
from jax.sharding import PartitionSpec as P

D = 8192
BLOCK = 512
HALF = BLOCK // 2
LANES = 128
DENSE_WINDOW = 2048


precise = lax.Precision.HIGHEST
full_turn = 6.283185307179586


def angles(first, second, period, offset):
    left_index = lax.broadcasted_iota(jnp.int32, (first, second), 0)
    right_index = lax.broadcasted_iota(jnp.int32, (first, second), 1) + offset
    return full_turn / period * (left_index * right_index % period).astype(jnp.float32)


def placed(table, layout):
    shape = []
    for letter in layout:
        if letter == "k":
            shape.append(table.shape[0])
        elif letter == "m":
            shape.append(table.shape[1])
        else:
            shape.append(1)
    return table.reshape(shape)


def contract(layout, values, table, source, target):
    result = layout.replace(source, target)
    return jnp.einsum(
        layout + "," + source + target + "->" + result, values, table, precision=precise
    )


def forward_outer(values, layout, offset, period):
    outer = values.shape[layout.index("p")]
    inner = values.shape[layout.index("m")]
    table = angles(outer, 2 * outer, 2 * outer, 0)
    widened = values.astype(jnp.float32)
    real_part = contract(layout, widened, jnp.cos(table), "p", "k")
    imag_part = -contract(layout, widened, jnp.sin(table), "p", "k")
    turned = layout.replace("p", "k")
    twist = angles(2 * outer, inner, period, offset)
    cosine = placed(jnp.cos(twist), turned)
    sine = placed(jnp.sin(twist), turned)
    return (real_part * cosine + imag_part * sine, imag_part * cosine - real_part * sine)


def forward_inner(real_part, imag_part, layout):
    inner = real_part.shape[layout.index("m")]
    table = angles(inner, inner, inner, 0)
    cosine = jnp.cos(table)
    sine = jnp.sin(table)
    new_real = contract(layout, real_part, cosine, "m", "n") + contract(
        layout, imag_part, sine, "m", "n"
    )
    new_imag = contract(layout, imag_part, cosine, "m", "n") - contract(
        layout, real_part, sine, "m", "n"
    )
    return (new_real, new_imag)


def inverse_inner(real_part, imag_part, layout):
    inner = real_part.shape[layout.index("m")]
    table = angles(inner, inner, inner, 0)
    cosine = jnp.cos(table)
    sine = jnp.sin(table)
    new_real = contract(layout, real_part, cosine, "m", "n") - contract(
        layout, imag_part, sine, "m", "n"
    )
    new_imag = contract(layout, imag_part, cosine, "m", "n") + contract(
        layout, real_part, sine, "m", "n"
    )
    return (new_real, new_imag)


def inverse_outer(real_part, imag_part, layout, offset, period):
    doubled = real_part.shape[layout.index("k")]
    inner = real_part.shape[layout.index("m")]
    twist = angles(doubled, inner, period, offset)
    cosine = placed(jnp.cos(twist), layout)
    sine = placed(jnp.sin(twist), layout)
    turned_real = real_part * cosine - imag_part * sine
    turned_imag = imag_part * cosine + real_part * sine
    table = angles(doubled, doubled // 2, doubled, 0)
    summed = contract(layout, turned_real, jnp.cos(table), "k", "p") - contract(
        layout, turned_imag, jnp.sin(table), "k", "p"
    )
    return summed / period


def spectral_product(real_part, imag_part):
    real_out = real_part[0] * real_part[1] - imag_part[0] * imag_part[1]
    imag_out = real_part[0] * imag_part[1] + imag_part[0] * real_part[1]
    return (real_out, imag_out)


def packed_dft(size, rows):
    half = size // 2
    turn = (np.arange(rows)[:, None] * np.arange(half)[None, :]) % size
    angle = 2.0 * np.pi / size * turn
    cosine = np.cos(angle)
    sine = -np.sin(angle)
    sine[:, 0] = 1.0 - 2.0 * (np.arange(rows) % 2)
    return cosine, sine


def packed_weights(size):
    half = size // 2
    weight = np.full((half,), 2.0 / size)
    weight[0] = 1.0 / size
    return weight


def block_tables():
    cosine, sine = packed_dft(BLOCK, BLOCK)
    forward = np.concatenate([cosine, sine], axis=1)
    weight = packed_weights(BLOCK)
    inverse = np.concatenate([cosine * weight, sine * weight], axis=1).T
    cross = sine.copy()
    cross[:, 0] = 0.0
    straight = cosine.copy()
    straight[:, 0] = sine[:, 0]
    taps = np.concatenate([cross, cosine + cross, straight - cross], axis=1)
    return (
        jnp.asarray(forward, jnp.bfloat16),
        jnp.asarray(inverse, jnp.bfloat16),
        jnp.asarray(taps, jnp.bfloat16),
    )


def short_window(both):
    length, width = both.shape[0], both.shape[1] // 2
    cosine, sine = packed_dft(2 * length, length)
    table = jnp.asarray(np.concatenate([cosine, sine], axis=1).T, jnp.bfloat16)
    spectrum = jnp.dot(table, both, preferred_element_type=jnp.float32)
    real_s, real_k = spectrum[:length, :width], spectrum[:length, width:]
    imag_s, imag_k = spectrum[length:, :width], spectrum[length:, width:]
    first = lax.broadcasted_iota(jnp.int32, (length, 1), 0) == 0
    weight = jnp.asarray(packed_weights(2 * length)[:, None], jnp.float32)
    crossed = imag_s * imag_k
    real_out = weight * (real_s * real_k - jnp.where(first, 0.0, crossed))
    imag_out = weight * jnp.where(first, crossed, real_s * imag_k + imag_s * real_k)
    product = jnp.concatenate([real_out, imag_out], axis=0).astype(jnp.bfloat16)
    return lax.dot_general(
        table, product, (((0,), (0,)), ((), ())), preferred_element_type=jnp.float32
    )


def long_window(signal, kernel, outer):
    period = 2 * signal.shape[0]
    tokens = signal.shape[0] // outer
    stacked = jnp.stack([signal, kernel]).reshape(2, outer, tokens, -1).transpose(0, 3, 1, 2)
    real_part, imag_part = forward_outer(stacked, "scpm", 0, period)
    real_part, imag_part = forward_inner(real_part, imag_part, "sckm")
    real_part, imag_part = spectral_product(real_part, imag_part)
    real_part, imag_part = inverse_inner(real_part, imag_part, "ckm")
    local_mixed = inverse_outer(real_part, imag_part, "ckm", 0, period)
    return local_mixed.transpose(1, 2, 0).reshape(outer * tokens, -1)


def mix_blocks(tokens, outs, ins, chunk, real_ref, imag_ref, sum_ref, w_ref, spec_ref, row_of):
    for half in range(HALF // LANES):
        lanes = pl.ds(half * LANES, LANES)

        @pl.loop(0, outs // 2)
        def _(pair):
            def step(part, totals):
                totals = list(totals)
                for inner in range(chunk):
                    if inner % 8 == 0:
                        held = [
                            [
                                w_ref[
                                    pl.ds(pl.multiple_of(row_of(pair * 2 + b, part, inner), 8), 8),
                                    k * HALF + half * LANES : k * HALF + (half + 1) * LANES,
                                ]
                                for k in range(3)
                            ]
                            for b in range(2)
                        ]
                    rows = pl.ds(pl.multiple_of((part * chunk + inner) * tokens, tokens), tokens)
                    real = real_ref[rows, lanes]
                    imag = imag_ref[rows, lanes]
                    both = sum_ref[rows, lanes]
                    at = inner % 8
                    for b in range(2):
                        w0, w1, w2 = [held[b][k][at : at + 1] for k in range(3)]
                        totals[3 * b] = totals[3 * b] + w0 * both
                        totals[3 * b + 1] = totals[3 * b + 1] + w1 * real
                        totals[3 * b + 2] = totals[3 * b + 2] + w2 * imag
                return tuple(totals)

            zero = jnp.zeros((tokens, LANES), jnp.float32)
            totals = (zero,) * 6
            if ins == chunk:
                totals = step(0, totals)
            else:
                totals = lax.fori_loop(0, ins // chunk, step, totals)
            for b in range(2):
                rows = pl.ds(pl.multiple_of((pair * 2 + b) * tokens, tokens), tokens)
                cross, real, imag = totals[3 * b : 3 * b + 3]
                spec_ref[rows, half * LANES : (half + 1) * LANES] = (real - cross).astype(
                    jnp.bfloat16
                )
                spec_ref[rows, HALF + half * LANES : HALF + (half + 1) * LANES] = (
                    cross + imag
                ).astype(jnp.bfloat16)


def mlp_kernel(
    local,
    mine_ref,
    cols_ref,
    fwd_ref,
    inv_ref,
    tap_ref,
    out_ref,
    x_ref,
    done_ref,
    w_ref,
    rows_ref,
    hid_ref,
    spec_ref,
    real_ref,
    imag_ref,
    sum_ref,
    send_sem,
    recv_sem,
    back_send_sem,
    back_recv_sem,
):
    groups, tokens, width = mine_ref.shape
    per_group = width // BLOCK
    ins = groups * per_group
    tiles = groups * local
    stride = 2 * local * ins
    held = cols_ref.shape[0] // groups
    me = lax.axis_index("tp")
    peers = [lax.rem(me + d, groups) for d in range(1, groups)]

    barrier = pltpu.get_barrier_semaphore()
    for peer in peers:
        pl.semaphore_signal(
            barrier, inc=1, device_id={"tp": peer}, device_id_type=pl.DeviceIdType.MESH
        )
    pl.semaphore_wait(barrier, groups - 1)

    def send(d, src, dst, sent, got):
        copy = pltpu.make_async_remote_copy(
            src_ref=src.at[peers[d]],
            dst_ref=dst.at[me],
            send_sem=sent.at[d],
            recv_sem=got.at[d],
            device_id={"tp": peers[d]},
            device_id_type=pl.DeviceIdType.MESH,
        )
        copy.start()
        return copy

    copies = [send(d, mine_ref, x_ref, send_sem, recv_sem) for d in range(groups - 1)]
    x_ref[me] = mine_ref[me]
    for p in range(groups):
        for part in range(2):
            at = part * local * ins
            w_ref[p * stride + at : p * stride + at + local * ins, :] = jnp.dot(
                cols_ref[p * held + at : p * held + at + local * ins, :],
                tap_ref[...],
                preferred_element_type=jnp.float32,
            )
    for copy in copies:
        copy.wait()

    squares = jnp.zeros((tokens, 1), jnp.float32)
    for p in range(groups):
        wide = x_ref[p].astype(jnp.float32)
        squares = squares + jnp.sum(wide * wide, axis=1, keepdims=True)
    scale = lax.rsqrt(squares / (groups * width) + 1e-06)
    for j in range(ins):
        p, at = j // per_group, (j % per_group) * BLOCK
        wide = x_ref[p, :, at : at + BLOCK].astype(jnp.float32)
        row = p * held + stride + j % per_group
        gain = cols_ref[row : row + 1, :].astype(jnp.float32)
        rows_ref[j * tokens : (j + 1) * tokens, :] = (wide * scale * gain).astype(jnp.bfloat16)

    piece = 256

    def forward(values_ref, total):
        @pl.loop(0, total // piece)
        def _(at):
            rows = pl.ds(pl.multiple_of(at * piece, piece), piece)
            spec = jnp.dot(values_ref[rows, :], fwd_ref[...], preferred_element_type=jnp.float32)
            real_ref[rows, :] = spec[:, :HALF]
            imag_ref[rows, :] = spec[:, HALF:]
            sum_ref[rows, :] = spec[:, :HALF] + spec[:, HALF:]

    forward(rows_ref, ins * tokens)

    def up_row(i, part, inner):
        return (i // local) * stride + (i % local) * ins + inner

    mix_blocks(tokens, tiles, ins, ins, real_ref, imag_ref, sum_ref, w_ref, spec_ref, up_row)

    @pl.loop(0, tiles * tokens // piece)
    def _(at):
        rows = pl.ds(pl.multiple_of(at * piece, piece), piece)
        pre = jnp.dot(spec_ref[rows, :], inv_ref[...], preferred_element_type=jnp.float32)
        hidden = 0.5 * pre * (1.0 + lax.erf(pre * math.sqrt(0.5)))
        hid_ref[rows, :] = hidden.astype(jnp.bfloat16)

    forward(hid_ref, tiles * tokens)

    copies = []
    for d in range(groups):
        target = peers[d] if d < groups - 1 else me

        def down_row(i, part, inner):
            return part * stride + local * ins + (target * per_group + i) * local + inner

        mix_blocks(
            tokens, per_group, tiles, local, real_ref, imag_ref, sum_ref, w_ref, spec_ref, down_row
        )
        branch = jnp.dot(
            spec_ref[: per_group * tokens, :], inv_ref[...], preferred_element_type=jnp.float32
        )
        for i in range(per_group):
            at = i * BLOCK
            wide = x_ref[target, :, at : at + BLOCK].astype(jnp.float32)
            total = (wide + branch[i * tokens : (i + 1) * tokens]).astype(jnp.bfloat16)
            if d < groups - 1:
                done_ref[target, :, at : at + BLOCK] = total
            else:
                out_ref[target, :, at : at + BLOCK] = total
        if d < groups - 1:
            copies.append(send(d, done_ref, out_ref, back_send_sem, back_recv_sem))
    for copy in copies:
        copy.wait()


def mlp(stream, columns, local, forward_table, inverse_table, tap_table):
    groups, tokens, width = stream.shape
    ins = groups * width // BLOCK
    total = groups * local * tokens
    wide = pltpu.VMEM((total, HALF), jnp.float32)
    arrivals = pltpu.SemaphoreType.DMA((groups - 1,))
    return pl.pallas_call(
        functools.partial(mlp_kernel, local),
        out_shape=jax.ShapeDtypeStruct(stream.shape, jnp.bfloat16),
        in_specs=[pl.BlockSpec(memory_space=pltpu.VMEM)] * 5,
        out_specs=pl.BlockSpec(memory_space=pltpu.VMEM),
        scratch_shapes=[
            pltpu.VMEM(stream.shape, jnp.bfloat16),
            pltpu.VMEM(stream.shape, jnp.bfloat16),
            pltpu.VMEM((2 * groups * local * ins, 3 * HALF), jnp.float32),
            pltpu.VMEM((ins * tokens, BLOCK), jnp.bfloat16),
            pltpu.VMEM((total, BLOCK), jnp.bfloat16),
            pltpu.VMEM((total, BLOCK), jnp.bfloat16),
            wide,
            wide,
            wide,
            arrivals,
            arrivals,
            arrivals,
            arrivals,
        ],
        compiler_params=pltpu.CompilerParams(
            vmem_limit_bytes=40 * 1024 * 1024, collective_id=1, has_side_effects=True
        ),
        name="circulant_mlp",
    )(stream, columns, forward_table, inverse_table, tap_table)


def body(
    token_ids,
    embed_table,
    query_feat,
    key_feat,
    value_feat,
    long_filter,
    skip_gain,
    norm_gain,
    circulant_up,
    circulant_down,
):
    tokens = token_ids.shape[0]
    vocab = embed_table.shape[0]
    outer = lax.axis_size("ctx")
    groups = lax.axis_size("tp")
    width = query_feat.shape[1]
    ins = circulant_up.shape[1]
    local = circulant_up.shape[0]
    gated_wide = key_feat.astype(jnp.float32) * value_feat.astype(jnp.float32)
    gated = gated_wide.astype(jnp.bfloat16)
    pairs = jnp.concatenate(
        [gated.reshape(tokens, outer, -1), long_filter.reshape(tokens, outer, -1)], axis=2
    )
    arrived = lax.all_to_all(pairs, "ctx", split_axis=1, concat_axis=0)
    arrived = arrived.reshape(outer * tokens, -1)
    forward_table, inverse_table, tap_table = block_tables()
    gain_rows = norm_gain.reshape(-1, BLOCK)
    padded = 32
    gain_rows = jnp.pad(gain_rows, ((0, padded - gain_rows.shape[0]), (0, 0)))
    columns = jnp.concatenate(
        [circulant_up.reshape(-1, BLOCK), circulant_down.reshape(-1, BLOCK), gain_rows], axis=0
    )
    share = columns.shape[0] // 2
    half_columns = lax.dynamic_slice_in_dim(columns, lax.axis_index("ctx") % 2 * share, share)
    half_gathered = lax.all_gather(half_columns, "tp", axis=0, tiled=False)
    onehot = (token_ids[:, None] == lax.broadcasted_iota(jnp.int32, (1, vocab), 1)).astype(
        jnp.bfloat16
    )
    embedded = jnp.dot(onehot, embed_table, preferred_element_type=jnp.float32)
    if outer * tokens <= DENSE_WINDOW:
        local_mixed = short_window(arrived)
    else:
        local_mixed = long_window(*jnp.split(arrived, 2, axis=1), outer)
    local_mixed = local_mixed.astype(jnp.bfloat16)
    half_gathered, local_mixed = lax.optimization_barrier((half_gathered, local_mixed))
    chips = [[2 * chip, 2 * chip + 1] for chip in range(outer // 2)]
    both_halves = lax.all_gather(
        half_gathered, "ctx", axis=0, tiled=False, axis_index_groups=chips
    )
    all_columns = both_halves.transpose(1, 0, 2, 3).reshape(-1, BLOCK)
    mixed = lax.all_to_all(
        local_mixed, "ctx", split_axis=0, concat_axis=1, tiled=True
    ).astype(jnp.float32)
    mixed = mixed + skip_gain[None, :] * gated.astype(jnp.float32)
    stream = (embedded + query_feat.astype(jnp.float32) * mixed).astype(jnp.bfloat16)
    own = stream.reshape(groups, tokens // groups, width)
    result = mlp(own, all_columns, local, forward_table, inverse_table, tap_table)
    return result.reshape(tokens, width)


def solution(mesh):
    placed = (
        P("ctx"),
        P(None, "tp"),
        P("ctx", "tp"),
        P("ctx", "tp"),
        P("ctx", "tp"),
        P("ctx", "tp"),
        P("tp"),
        P("tp"),
        P("tp", None, None),
        P(None, "tp", None),
    )
    return jax.shard_map(
        body, mesh=mesh, in_specs=placed, out_specs=P("ctx", "tp"), check_vma=False
    )
```

```python
import functools
import math

import jax
import jax.numpy as jnp
import numpy as np
from jax import lax
from jax.experimental import pallas as pl
from jax.experimental.pallas import tpu as pltpu
from jax.sharding import PartitionSpec as P

D = 8192
BLOCK = 512
HALF = BLOCK // 2
LANES = 128
DENSE_WINDOW = 2048


precise = lax.Precision.HIGHEST
full_turn = 6.283185307179586


def angles(first, second, period, offset):
    left_index = lax.broadcasted_iota(jnp.int32, (first, second), 0)
    right_index = lax.broadcasted_iota(jnp.int32, (first, second), 1) + offset
    return full_turn / period * (left_index * right_index % period).astype(jnp.float32)


def placed(table, layout):
    shape = []
    for letter in layout:
        if letter == "k":
            shape.append(table.shape[0])
        elif letter == "m":
            shape.append(table.shape[1])
        else:
            shape.append(1)
    return table.reshape(shape)


def contract(layout, values, table, source, target):
    result = layout.replace(source, target)
    return jnp.einsum(
        layout + "," + source + target + "->" + result, values, table, precision=precise
    )


def forward_outer(values, layout, offset, period):
    outer = values.shape[layout.index("p")]
    inner = values.shape[layout.index("m")]
    table = angles(outer, 2 * outer, 2 * outer, 0)
    widened = values.astype(jnp.float32)
    real_part = contract(layout, widened, jnp.cos(table), "p", "k")
    imag_part = -contract(layout, widened, jnp.sin(table), "p", "k")
    turned = layout.replace("p", "k")
    twist = angles(2 * outer, inner, period, offset)
    cosine = placed(jnp.cos(twist), turned)
    sine = placed(jnp.sin(twist), turned)
    return (real_part * cosine + imag_part * sine, imag_part * cosine - real_part * sine)


def forward_inner(real_part, imag_part, layout):
    inner = real_part.shape[layout.index("m")]
    table = angles(inner, inner, inner, 0)
    cosine = jnp.cos(table)
    sine = jnp.sin(table)
    new_real = contract(layout, real_part, cosine, "m", "n") + contract(
        layout, imag_part, sine, "m", "n"
    )
    new_imag = contract(layout, imag_part, cosine, "m", "n") - contract(
        layout, real_part, sine, "m", "n"
    )
    return (new_real, new_imag)


def inverse_inner(real_part, imag_part, layout):
    inner = real_part.shape[layout.index("m")]
    table = angles(inner, inner, inner, 0)
    cosine = jnp.cos(table)
    sine = jnp.sin(table)
    new_real = contract(layout, real_part, cosine, "m", "n") - contract(
        layout, imag_part, sine, "m", "n"
    )
    new_imag = contract(layout, imag_part, cosine, "m", "n") + contract(
        layout, real_part, sine, "m", "n"
    )
    return (new_real, new_imag)


def inverse_outer(real_part, imag_part, layout, offset, period):
    doubled = real_part.shape[layout.index("k")]
    inner = real_part.shape[layout.index("m")]
    twist = angles(doubled, inner, period, offset)
    cosine = placed(jnp.cos(twist), layout)
    sine = placed(jnp.sin(twist), layout)
    turned_real = real_part * cosine - imag_part * sine
    turned_imag = imag_part * cosine + real_part * sine
    table = angles(doubled, doubled // 2, doubled, 0)
    summed = contract(layout, turned_real, jnp.cos(table), "k", "p") - contract(
        layout, turned_imag, jnp.sin(table), "k", "p"
    )
    return summed / period


def spectral_product(real_part, imag_part):
    real_out = real_part[0] * real_part[1] - imag_part[0] * imag_part[1]
    imag_out = real_part[0] * imag_part[1] + imag_part[0] * real_part[1]
    return (real_out, imag_out)


def packed_dft(size, rows):
    half = size // 2
    turn = (np.arange(rows)[:, None] * np.arange(half)[None, :]) % size
    angle = 2.0 * np.pi / size * turn
    cosine = np.cos(angle)
    sine = -np.sin(angle)
    sine[:, 0] = 1.0 - 2.0 * (np.arange(rows) % 2)
    return cosine, sine


def packed_weights(size):
    half = size // 2
    weight = np.full((half,), 2.0 / size)
    weight[0] = 1.0 / size
    return weight


def block_tables():
    cosine, sine = packed_dft(BLOCK, BLOCK)
    forward = np.concatenate([cosine, sine], axis=1)
    weight = packed_weights(BLOCK)
    inverse = np.concatenate([cosine * weight, sine * weight], axis=1).T
    cross = sine.copy()
    cross[:, 0] = 0.0
    straight = cosine.copy()
    straight[:, 0] = sine[:, 0]
    taps = np.concatenate([cross, cosine + cross, straight - cross], axis=1)
    return (
        jnp.asarray(forward, jnp.bfloat16),
        jnp.asarray(inverse, jnp.bfloat16),
        jnp.asarray(taps, jnp.bfloat16),
    )


def conv_kernel(
    key_ref,
    value_ref,
    filter_ref,
    fwd_ref,
    inv_ref,
    cols_ref,
    mixed_ref,
    gated_ref,
    all_ref,
    both_ref,
    spec_ref,
    prod_ref,
    loc_ref,
    out_sem,
    in_sem,
    back_out_sem,
    back_in_sem,
    z_out_sem,
    z_in_sem,
    pair_out_sem,
    pair_in_sem,
):
    tokens = key_ref.shape[0]
    length = both_ref.shape[0]
    width = prod_ref.shape[1]
    outer = length // tokens
    groups, held = all_ref.shape[0], all_ref.shape[1]
    share = held // 2
    me = lax.axis_index("ctx")
    row = lax.axis_index("tp")
    core = lax.rem(me, 2)
    sibling = me + 1 - 2 * core
    peers = [lax.rem(me + d, outer) for d in range(1, outer)]
    above = [lax.rem(row + d, groups) for d in range(1, groups)]
    below = [lax.rem(row + groups - d, groups) for d in range(1, groups)]
    mesh_type = pl.DeviceIdType.MESH

    gated_ref[...] = (
        key_ref[...].astype(jnp.float32) * value_ref[...].astype(jnp.float32)
    ).astype(jnp.bfloat16)

    barrier = pltpu.get_barrier_semaphore()
    for peer in peers:
        pl.semaphore_signal(barrier, inc=1, device_id={"ctx": peer}, device_id_type=mesh_type)
    for peer in above:
        pl.semaphore_signal(barrier, inc=1, device_id={"tp": peer}, device_id_type=mesh_type)
    pl.semaphore_wait(barrier, outer + groups - 2)

    def send(src, dst, sent, got, target):
        copy = pltpu.make_async_remote_copy(
            src_ref=src,
            dst_ref=dst,
            send_sem=sent,
            recv_sem=got,
            device_id=target,
            device_id_type=mesh_type,
        )
        copy.start()
        return copy

    def positions(at):
        return pl.ds(pl.multiple_of(at * tokens, tokens), tokens)

    def channels(at):
        return pl.ds(pl.multiple_of(at * width, width), width)

    copies = []
    for d, peer in enumerate(peers):
        for part, src in enumerate((gated_ref, filter_ref)):
            copies.append(
                send(
                    src.at[:, channels(peer)],
                    both_ref.at[positions(me), pl.ds(part * width, width)],
                    out_sem.at[d, part],
                    in_sem.at[d, part],
                    {"ctx": peer},
                )
            )
    half = pl.ds(pl.multiple_of(core * share, share), share)
    z_copies = [
        send(
            cols_ref.at[half], all_ref.at[row, half], z_out_sem.at[d], z_in_sem.at[d], {"tp": peer}
        )
        for d, peer in enumerate(above)
    ]
    all_ref[row] = cols_ref[...]
    both_ref[positions(me), :width] = gated_ref[:, channels(me)]
    both_ref[positions(me), width:] = filter_ref[:, channels(me)]
    for copy in copies:
        copy.wait()

    piece = 256

    @pl.loop(0, 2 * length // piece)
    def _(at):
        rows = pl.ds(pl.multiple_of(at * piece, piece), piece)
        spec_ref[rows, :] = jnp.dot(
            fwd_ref[rows, :], both_ref[...], preferred_element_type=jnp.float32
        )

    size = 2 * length

    @pl.loop(0, length // LANES)
    def _(at):
        real = pl.ds(pl.multiple_of(at * LANES, LANES), LANES)
        imag = pl.ds(pl.multiple_of(length + at * LANES, LANES), LANES)
        real_s, real_k = spec_ref[real, :width], spec_ref[real, width:]
        imag_s, imag_k = spec_ref[imag, :width], spec_ref[imag, width:]
        first = lax.broadcasted_iota(jnp.int32, (LANES, width), 0) + at * LANES == 0
        weight = jnp.where(first, 1.0 / size, 2.0 / size)
        crossed = imag_s * imag_k
        straight = real_s * real_k
        mixed_terms = real_s * imag_k + imag_s * real_k
        prod_ref[real, :] = (weight * (straight - jnp.where(first, 0.0, crossed))).astype(
            jnp.bfloat16
        )
        prod_ref[imag, :] = (weight * jnp.where(first, crossed, mixed_terms)).astype(jnp.bfloat16)

    copies = []
    for d in range(outer):
        target = peers[d] if d < outer - 1 else me
        values = jnp.dot(
            inv_ref[positions(target), :], prod_ref[...], preferred_element_type=jnp.float32
        ).astype(jnp.bfloat16)
        if d < outer - 1:
            loc_ref[positions(target), :] = values
            copies.append(
                send(
                    loc_ref.at[positions(target)],
                    mixed_ref.at[:, channels(me)],
                    back_out_sem.at[d],
                    back_in_sem.at[d],
                    {"ctx": target},
                )
            )
        else:
            mixed_ref[:, channels(me)] = values
    for copy in z_copies:
        copy.wait()
    for d, source in enumerate(below):
        copies.append(
            send(
                all_ref.at[source, half],
                all_ref.at[source, half],
                pair_out_sem.at[d],
                pair_in_sem.at[d],
                {"ctx": sibling},
            )
        )
    for copy in copies:
        copy.wait()


def short_window(key_feat, value_feat, long_filter, columns, outer, groups):
    tokens, channels = key_feat.shape
    length, width = outer * tokens, channels // outer
    cosine, sine = packed_dft(2 * length, length)
    table = np.concatenate([cosine, sine], axis=1)
    vmem = pl.BlockSpec(memory_space=pltpu.VMEM)
    dma = pltpu.SemaphoreType.DMA
    return pl.pallas_call(
        conv_kernel,
        out_shape=(
            jax.ShapeDtypeStruct(key_feat.shape, jnp.bfloat16),
            jax.ShapeDtypeStruct(key_feat.shape, jnp.bfloat16),
            jax.ShapeDtypeStruct((groups,) + columns.shape, jnp.bfloat16),
        ),
        in_specs=[vmem] * 6,
        out_specs=(vmem,) * 3,
        scratch_shapes=[
            pltpu.VMEM((length, 2 * width), jnp.bfloat16),
            pltpu.VMEM((2 * length, 2 * width), jnp.float32),
            pltpu.VMEM((2 * length, width), jnp.bfloat16),
            pltpu.VMEM((length, width), jnp.bfloat16),
            dma((outer - 1, 2)),
            dma((outer - 1, 2)),
            dma((outer - 1,)),
            dma((outer - 1,)),
            dma((groups - 1,)),
            dma((groups - 1,)),
            dma((groups - 1,)),
            dma((groups - 1,)),
        ],
        compiler_params=pltpu.CompilerParams(
            vmem_limit_bytes=40 * 1024 * 1024, collective_id=2, has_side_effects=True
        ),
        name="long_conv",
    )(
        key_feat,
        value_feat,
        long_filter,
        jnp.asarray(table.T, jnp.bfloat16),
        jnp.asarray(table, jnp.bfloat16),
        columns,
    )


def long_window(signal, kernel, outer):
    period = 2 * signal.shape[0]
    tokens = signal.shape[0] // outer
    stacked = jnp.stack([signal, kernel]).reshape(2, outer, tokens, -1).transpose(0, 3, 1, 2)
    real_part, imag_part = forward_outer(stacked, "scpm", 0, period)
    real_part, imag_part = forward_inner(real_part, imag_part, "sckm")
    real_part, imag_part = spectral_product(real_part, imag_part)
    real_part, imag_part = inverse_inner(real_part, imag_part, "ckm")
    local_mixed = inverse_outer(real_part, imag_part, "ckm", 0, period)
    return local_mixed.transpose(1, 2, 0).reshape(outer * tokens, -1)


def mix_blocks(tokens, outs, ins, chunk, real_ref, imag_ref, sum_ref, w_ref, spec_ref, row_of):
    for half in range(HALF // LANES):
        lanes = pl.ds(half * LANES, LANES)

        @pl.loop(0, outs // 2)
        def _(pair):
            def step(part, totals):
                totals = list(totals)
                for inner in range(chunk):
                    if inner % 8 == 0:
                        held = [
                            [
                                w_ref[
                                    pl.ds(pl.multiple_of(row_of(pair * 2 + b, part, inner), 8), 8),
                                    k * HALF + half * LANES : k * HALF + (half + 1) * LANES,
                                ]
                                for k in range(3)
                            ]
                            for b in range(2)
                        ]
                    rows = pl.ds(pl.multiple_of((part * chunk + inner) * tokens, tokens), tokens)
                    real = real_ref[rows, lanes]
                    imag = imag_ref[rows, lanes]
                    both = sum_ref[rows, lanes]
                    at = inner % 8
                    for b in range(2):
                        w0, w1, w2 = [held[b][k][at : at + 1] for k in range(3)]
                        totals[3 * b] = totals[3 * b] + w0 * both
                        totals[3 * b + 1] = totals[3 * b + 1] + w1 * real
                        totals[3 * b + 2] = totals[3 * b + 2] + w2 * imag
                return tuple(totals)

            zero = jnp.zeros((tokens, LANES), jnp.float32)
            totals = (zero,) * 6
            if ins == chunk:
                totals = step(0, totals)
            else:
                totals = lax.fori_loop(0, ins // chunk, step, totals)
            for b in range(2):
                rows = pl.ds(pl.multiple_of((pair * 2 + b) * tokens, tokens), tokens)
                cross, real, imag = totals[3 * b : 3 * b + 3]
                spec_ref[rows, half * LANES : (half + 1) * LANES] = (real - cross).astype(
                    jnp.bfloat16
                )
                spec_ref[rows, HALF + half * LANES : HALF + (half + 1) * LANES] = (
                    cross + imag
                ).astype(jnp.bfloat16)


def mlp_kernel(
    local,
    mine_ref,
    cols_ref,
    fwd_ref,
    inv_ref,
    tap_ref,
    out_ref,
    x_ref,
    done_ref,
    w_ref,
    rows_ref,
    hid_ref,
    spec_ref,
    real_ref,
    imag_ref,
    sum_ref,
    send_sem,
    recv_sem,
    back_send_sem,
    back_recv_sem,
):
    groups, tokens, width = mine_ref.shape
    per_group = width // BLOCK
    ins = groups * per_group
    tiles = groups * local
    stride = 2 * local * ins
    held = cols_ref.shape[0] // groups
    me = lax.axis_index("tp")
    peers = [lax.rem(me + d, groups) for d in range(1, groups)]

    barrier = pltpu.get_barrier_semaphore()
    for peer in peers:
        pl.semaphore_signal(
            barrier, inc=1, device_id={"tp": peer}, device_id_type=pl.DeviceIdType.MESH
        )
    pl.semaphore_wait(barrier, groups - 1)

    def send(d, src, dst, sent, got):
        copy = pltpu.make_async_remote_copy(
            src_ref=src.at[peers[d]],
            dst_ref=dst.at[me],
            send_sem=sent.at[d],
            recv_sem=got.at[d],
            device_id={"tp": peers[d]},
            device_id_type=pl.DeviceIdType.MESH,
        )
        copy.start()
        return copy

    copies = [send(d, mine_ref, x_ref, send_sem, recv_sem) for d in range(groups - 1)]
    x_ref[me] = mine_ref[me]
    for p in range(groups):
        for part in range(2):
            at = part * local * ins
            w_ref[p * stride + at : p * stride + at + local * ins, :] = jnp.dot(
                cols_ref[p * held + at : p * held + at + local * ins, :],
                tap_ref[...],
                preferred_element_type=jnp.float32,
            )
    for copy in copies:
        copy.wait()

    squares = jnp.zeros((tokens, 1), jnp.float32)
    for p in range(groups):
        wide = x_ref[p].astype(jnp.float32)
        squares = squares + jnp.sum(wide * wide, axis=1, keepdims=True)
    scale = lax.rsqrt(squares / (groups * width) + 1e-06)
    for j in range(ins):
        p, at = j // per_group, (j % per_group) * BLOCK
        wide = x_ref[p, :, at : at + BLOCK].astype(jnp.float32)
        row = p * held + stride + j % per_group
        gain = cols_ref[row : row + 1, :].astype(jnp.float32)
        rows_ref[j * tokens : (j + 1) * tokens, :] = (wide * scale * gain).astype(jnp.bfloat16)

    piece = 256

    def forward(values_ref, total):
        @pl.loop(0, total // piece)
        def _(at):
            rows = pl.ds(pl.multiple_of(at * piece, piece), piece)
            spec = jnp.dot(values_ref[rows, :], fwd_ref[...], preferred_element_type=jnp.float32)
            real_ref[rows, :] = spec[:, :HALF]
            imag_ref[rows, :] = spec[:, HALF:]
            sum_ref[rows, :] = spec[:, :HALF] + spec[:, HALF:]

    forward(rows_ref, ins * tokens)

    def up_row(i, part, inner):
        return (i // local) * stride + (i % local) * ins + inner

    mix_blocks(tokens, tiles, ins, ins, real_ref, imag_ref, sum_ref, w_ref, spec_ref, up_row)

    @pl.loop(0, tiles * tokens // piece)
    def _(at):
        rows = pl.ds(pl.multiple_of(at * piece, piece), piece)
        pre = jnp.dot(spec_ref[rows, :], inv_ref[...], preferred_element_type=jnp.float32)
        hidden = 0.5 * pre * (1.0 + lax.erf(pre * math.sqrt(0.5)))
        hid_ref[rows, :] = hidden.astype(jnp.bfloat16)

    forward(hid_ref, tiles * tokens)

    copies = []
    for d in range(groups):
        target = peers[d] if d < groups - 1 else me

        def down_row(i, part, inner):
            return part * stride + local * ins + (target * per_group + i) * local + inner

        mix_blocks(
            tokens, per_group, tiles, local, real_ref, imag_ref, sum_ref, w_ref, spec_ref, down_row
        )
        branch = jnp.dot(
            spec_ref[: per_group * tokens, :], inv_ref[...], preferred_element_type=jnp.float32
        )
        for i in range(per_group):
            at = i * BLOCK
            wide = x_ref[target, :, at : at + BLOCK].astype(jnp.float32)
            total = (wide + branch[i * tokens : (i + 1) * tokens]).astype(jnp.bfloat16)
            if d < groups - 1:
                done_ref[target, :, at : at + BLOCK] = total
            else:
                out_ref[target, :, at : at + BLOCK] = total
        if d < groups - 1:
            copies.append(send(d, done_ref, out_ref, back_send_sem, back_recv_sem))
    for copy in copies:
        copy.wait()


def mlp(stream, columns, local, forward_table, inverse_table, tap_table):
    groups, tokens, width = stream.shape
    ins = groups * width // BLOCK
    total = groups * local * tokens
    wide = pltpu.VMEM((total, HALF), jnp.float32)
    arrivals = pltpu.SemaphoreType.DMA((groups - 1,))
    return pl.pallas_call(
        functools.partial(mlp_kernel, local),
        out_shape=jax.ShapeDtypeStruct(stream.shape, jnp.bfloat16),
        in_specs=[pl.BlockSpec(memory_space=pltpu.VMEM)] * 5,
        out_specs=pl.BlockSpec(memory_space=pltpu.VMEM),
        scratch_shapes=[
            pltpu.VMEM(stream.shape, jnp.bfloat16),
            pltpu.VMEM(stream.shape, jnp.bfloat16),
            pltpu.VMEM((2 * groups * local * ins, 3 * HALF), jnp.float32),
            pltpu.VMEM((ins * tokens, BLOCK), jnp.bfloat16),
            pltpu.VMEM((total, BLOCK), jnp.bfloat16),
            pltpu.VMEM((total, BLOCK), jnp.bfloat16),
            wide,
            wide,
            wide,
            arrivals,
            arrivals,
            arrivals,
            arrivals,
        ],
        compiler_params=pltpu.CompilerParams(
            vmem_limit_bytes=40 * 1024 * 1024, collective_id=1, has_side_effects=True
        ),
        name="circulant_mlp",
    )(stream, columns, forward_table, inverse_table, tap_table)


def body(
    token_ids,
    embed_table,
    query_feat,
    key_feat,
    value_feat,
    long_filter,
    skip_gain,
    norm_gain,
    circulant_up,
    circulant_down,
):
    tokens = token_ids.shape[0]
    vocab = embed_table.shape[0]
    outer = lax.axis_size("ctx")
    groups = lax.axis_size("tp")
    width = query_feat.shape[1]
    ins = circulant_up.shape[1]
    local = circulant_up.shape[0]
    forward_table, inverse_table, tap_table = block_tables()
    gain_rows = norm_gain.reshape(-1, BLOCK)
    padded = 32
    gain_rows = jnp.pad(gain_rows, ((0, padded - gain_rows.shape[0]), (0, 0)))
    columns = jnp.concatenate(
        [circulant_up.reshape(-1, BLOCK), circulant_down.reshape(-1, BLOCK), gain_rows], axis=0
    )
    onehot = (token_ids[:, None] == lax.broadcasted_iota(jnp.int32, (1, vocab), 1)).astype(
        jnp.bfloat16
    )
    embedded = jnp.dot(onehot, embed_table, preferred_element_type=jnp.float32)
    if 2 * outer * tokens <= DENSE_WINDOW and width // outer % LANES == 0:
        mixed, gated, all_columns = short_window(
            key_feat, value_feat, long_filter, columns, outer, groups
        )
        all_columns = all_columns.reshape(-1, BLOCK)
        mixed = mixed.astype(jnp.float32)
    else:
        gated_wide = key_feat.astype(jnp.float32) * value_feat.astype(jnp.float32)
        gated = gated_wide.astype(jnp.bfloat16)
        pairs = jnp.concatenate(
            [gated.reshape(tokens, outer, -1), long_filter.reshape(tokens, outer, -1)], axis=2
        )
        arrived = lax.all_to_all(pairs, "ctx", split_axis=1, concat_axis=0)
        arrived = arrived.reshape(outer * tokens, -1)
        all_columns = lax.all_gather(columns, "tp", axis=0, tiled=True)
        local_mixed = long_window(*jnp.split(arrived, 2, axis=1), outer)
        mixed = lax.all_to_all(
            local_mixed.astype(jnp.bfloat16), "ctx", split_axis=0, concat_axis=1, tiled=True
        ).astype(jnp.float32)
    mixed = mixed + skip_gain[None, :] * gated.astype(jnp.float32)
    stream = (embedded + query_feat.astype(jnp.float32) * mixed).astype(jnp.bfloat16)
    own = stream.reshape(groups, tokens // groups, width)
    result = mlp(own, all_columns, local, forward_table, inverse_table, tap_table)
    return result.reshape(tokens, width)


def solution(mesh):
    placed = (
        P("ctx"),
        P(None, "tp"),
        P("ctx", "tp"),
        P("ctx", "tp"),
        P("ctx", "tp"),
        P("ctx", "tp"),
        P("tp"),
        P("tp"),
        P("tp", None, None),
        P(None, "tp", None),
    )
    return jax.shard_map(
        body, mesh=mesh, in_specs=placed, out_specs=P("ctx", "tp"), check_vma=False
    )
```

```python
import functools
import math

import jax
import jax.numpy as jnp
import numpy as np
from jax import lax
from jax.experimental import pallas as pl
from jax.experimental.pallas import tpu as pltpu
from jax.sharding import PartitionSpec as P

D = 8192
BLOCK = 512
HALF = BLOCK // 2
LANES = 128
DENSE_WINDOW = 2048


precise = lax.Precision.HIGHEST
full_turn = 6.283185307179586


def angles(first, second, period, offset):
    left_index = lax.broadcasted_iota(jnp.int32, (first, second), 0)
    right_index = lax.broadcasted_iota(jnp.int32, (first, second), 1) + offset
    return full_turn / period * (left_index * right_index % period).astype(jnp.float32)


def placed(table, layout):
    shape = []
    for letter in layout:
        if letter == "k":
            shape.append(table.shape[0])
        elif letter == "m":
            shape.append(table.shape[1])
        else:
            shape.append(1)
    return table.reshape(shape)


def contract(layout, values, table, source, target):
    result = layout.replace(source, target)
    return jnp.einsum(
        layout + "," + source + target + "->" + result, values, table, precision=precise
    )


def forward_outer(values, layout, offset, period):
    outer = values.shape[layout.index("p")]
    inner = values.shape[layout.index("m")]
    table = angles(outer, 2 * outer, 2 * outer, 0)
    widened = values.astype(jnp.float32)
    real_part = contract(layout, widened, jnp.cos(table), "p", "k")
    imag_part = -contract(layout, widened, jnp.sin(table), "p", "k")
    turned = layout.replace("p", "k")
    twist = angles(2 * outer, inner, period, offset)
    cosine = placed(jnp.cos(twist), turned)
    sine = placed(jnp.sin(twist), turned)
    return (real_part * cosine + imag_part * sine, imag_part * cosine - real_part * sine)


def forward_inner(real_part, imag_part, layout):
    inner = real_part.shape[layout.index("m")]
    table = angles(inner, inner, inner, 0)
    cosine = jnp.cos(table)
    sine = jnp.sin(table)
    new_real = contract(layout, real_part, cosine, "m", "n") + contract(
        layout, imag_part, sine, "m", "n"
    )
    new_imag = contract(layout, imag_part, cosine, "m", "n") - contract(
        layout, real_part, sine, "m", "n"
    )
    return (new_real, new_imag)


def inverse_inner(real_part, imag_part, layout):
    inner = real_part.shape[layout.index("m")]
    table = angles(inner, inner, inner, 0)
    cosine = jnp.cos(table)
    sine = jnp.sin(table)
    new_real = contract(layout, real_part, cosine, "m", "n") - contract(
        layout, imag_part, sine, "m", "n"
    )
    new_imag = contract(layout, imag_part, cosine, "m", "n") + contract(
        layout, real_part, sine, "m", "n"
    )
    return (new_real, new_imag)


def inverse_outer(real_part, imag_part, layout, offset, period):
    doubled = real_part.shape[layout.index("k")]
    inner = real_part.shape[layout.index("m")]
    twist = angles(doubled, inner, period, offset)
    cosine = placed(jnp.cos(twist), layout)
    sine = placed(jnp.sin(twist), layout)
    turned_real = real_part * cosine - imag_part * sine
    turned_imag = imag_part * cosine + real_part * sine
    table = angles(doubled, doubled // 2, doubled, 0)
    summed = contract(layout, turned_real, jnp.cos(table), "k", "p") - contract(
        layout, turned_imag, jnp.sin(table), "k", "p"
    )
    return summed / period


def spectral_product(real_part, imag_part):
    real_out = real_part[0] * real_part[1] - imag_part[0] * imag_part[1]
    imag_out = real_part[0] * imag_part[1] + imag_part[0] * real_part[1]
    return (real_out, imag_out)


def packed_dft(size, rows):
    half = size // 2
    turn = (np.arange(rows)[:, None] * np.arange(half)[None, :]) % size
    angle = 2.0 * np.pi / size * turn
    cosine = np.cos(angle)
    sine = -np.sin(angle)
    sine[:, 0] = 1.0 - 2.0 * (np.arange(rows) % 2)
    return cosine, sine


def packed_weights(size):
    half = size // 2
    weight = np.full((half,), 2.0 / size)
    weight[0] = 1.0 / size
    return weight


def block_tables():
    cosine, sine = packed_dft(BLOCK, BLOCK)
    forward = np.concatenate([cosine, sine], axis=1)
    weight = packed_weights(BLOCK)
    inverse = np.concatenate([cosine * weight, sine * weight], axis=1).T
    cross = sine.copy()
    cross[:, 0] = 0.0
    straight = cosine.copy()
    straight[:, 0] = sine[:, 0]
    taps = np.concatenate([cross, cosine + cross, straight - cross], axis=1)
    return (
        jnp.asarray(forward, jnp.bfloat16),
        jnp.asarray(inverse, jnp.bfloat16),
        jnp.asarray(taps, jnp.bfloat16),
    )


def conv_kernel(
    key_ref,
    value_ref,
    filter_ref,
    fwd_hbm,
    inv_hbm,
    cols_ref,
    mixed_ref,
    gated_ref,
    all_ref,
    both_ref,
    spec_ref,
    prod_ref,
    loc_ref,
    fwd_ref,
    inv_ref,
    table_sem,
    out_sem,
    in_sem,
    back_out_sem,
    back_in_sem,
    z_out_sem,
    z_in_sem,
    pair_out_sem,
    pair_in_sem,
):
    tokens = key_ref.shape[0]
    length = both_ref.shape[0]
    width = prod_ref.shape[1]
    outer = length // tokens
    groups, held = all_ref.shape[0], all_ref.shape[1]
    share = held // 2
    me = lax.axis_index("ctx")
    row = lax.axis_index("tp")
    core = lax.rem(me, 2)
    sibling = me + 1 - 2 * core
    peers = [lax.rem(me + d, outer) for d in range(1, outer)]
    above = [lax.rem(row + d, groups) for d in range(1, groups)]
    below = [lax.rem(row + groups - d, groups) for d in range(1, groups)]
    mesh_type = pl.DeviceIdType.MESH

    fwd_copy = pltpu.make_async_copy(fwd_hbm, fwd_ref, table_sem.at[0])
    inv_copy = pltpu.make_async_copy(inv_hbm, inv_ref, table_sem.at[1])
    fwd_copy.start()
    inv_copy.start()
    gated_ref[...] = (
        key_ref[...].astype(jnp.float32) * value_ref[...].astype(jnp.float32)
    ).astype(jnp.bfloat16)

    barrier = pltpu.get_barrier_semaphore()
    for peer in peers:
        pl.semaphore_signal(barrier, inc=1, device_id={"ctx": peer}, device_id_type=mesh_type)
    for peer in above:
        pl.semaphore_signal(barrier, inc=1, device_id={"tp": peer}, device_id_type=mesh_type)
    pl.semaphore_wait(barrier, outer + groups - 2)

    def send(src, dst, sent, got, target):
        copy = pltpu.make_async_remote_copy(
            src_ref=src,
            dst_ref=dst,
            send_sem=sent,
            recv_sem=got,
            device_id=target,
            device_id_type=mesh_type,
        )
        copy.start()
        return copy

    def positions(at):
        return pl.ds(pl.multiple_of(at * tokens, tokens), tokens)

    def channels(at):
        return pl.ds(pl.multiple_of(at * width, width), width)

    copies = []
    for d, peer in enumerate(peers):
        for part, src in enumerate((gated_ref, filter_ref)):
            copies.append(
                send(
                    src.at[:, channels(peer)],
                    both_ref.at[positions(me), pl.ds(part * width, width)],
                    out_sem.at[d, part],
                    in_sem.at[d, part],
                    {"ctx": peer},
                )
            )
    half = pl.ds(pl.multiple_of(core * share, share), share)
    z_copies = [
        send(
            cols_ref.at[half], all_ref.at[row, half], z_out_sem.at[d], z_in_sem.at[d], {"tp": peer}
        )
        for d, peer in enumerate(above)
    ]
    all_ref[row] = cols_ref[...]
    both_ref[positions(me), :width] = gated_ref[:, channels(me)]
    both_ref[positions(me), width:] = filter_ref[:, channels(me)]
    for copy in copies:
        copy.wait()
    fwd_copy.wait()
    inv_copy.wait()

    piece = 256

    @pl.loop(0, 2 * length // piece)
    def _(at):
        rows = pl.ds(pl.multiple_of(at * piece, piece), piece)
        spec_ref[rows, :] = jnp.dot(
            fwd_ref[rows, :], both_ref[...], preferred_element_type=jnp.float32
        )

    size = 2 * length

    @pl.loop(0, length // LANES)
    def _(at):
        real = pl.ds(pl.multiple_of(at * LANES, LANES), LANES)
        imag = pl.ds(pl.multiple_of(length + at * LANES, LANES), LANES)
        real_s, real_k = spec_ref[real, :width], spec_ref[real, width:]
        imag_s, imag_k = spec_ref[imag, :width], spec_ref[imag, width:]
        first = lax.broadcasted_iota(jnp.int32, (LANES, width), 0) + at * LANES == 0
        weight = jnp.where(first, 1.0 / size, 2.0 / size)
        crossed = imag_s * imag_k
        straight = real_s * real_k
        mixed_terms = real_s * imag_k + imag_s * real_k
        prod_ref[real, :] = (weight * (straight - jnp.where(first, 0.0, crossed))).astype(
            jnp.bfloat16
        )
        prod_ref[imag, :] = (weight * jnp.where(first, crossed, mixed_terms)).astype(jnp.bfloat16)

    copies = []
    for d in range(outer):
        target = peers[d] if d < outer - 1 else me
        values = jnp.dot(
            inv_ref[positions(target), :], prod_ref[...], preferred_element_type=jnp.float32
        ).astype(jnp.bfloat16)
        if d < outer - 1:
            loc_ref[positions(target), :] = values
            copies.append(
                send(
                    loc_ref.at[positions(target)],
                    mixed_ref.at[:, channels(me)],
                    back_out_sem.at[d],
                    back_in_sem.at[d],
                    {"ctx": target},
                )
            )
        else:
            mixed_ref[:, channels(me)] = values
    for copy in z_copies:
        copy.wait()
    for d, source in enumerate(below):
        copies.append(
            send(
                all_ref.at[source, half],
                all_ref.at[source, half],
                pair_out_sem.at[d],
                pair_in_sem.at[d],
                {"ctx": sibling},
            )
        )
    for copy in copies:
        copy.wait()


def short_window(key_feat, value_feat, long_filter, columns, outer, groups):
    tokens, channels = key_feat.shape
    length, width = outer * tokens, channels // outer
    cosine, sine = packed_dft(2 * length, length)
    table = np.concatenate([cosine, sine], axis=1)
    vmem = pl.BlockSpec(memory_space=pltpu.VMEM)
    hbm = pl.BlockSpec(memory_space=pltpu.HBM)
    dma = pltpu.SemaphoreType.DMA
    return pl.pallas_call(
        conv_kernel,
        out_shape=(
            jax.ShapeDtypeStruct(key_feat.shape, jnp.bfloat16),
            jax.ShapeDtypeStruct(key_feat.shape, jnp.bfloat16),
            jax.ShapeDtypeStruct((groups,) + columns.shape, jnp.bfloat16),
        ),
        in_specs=[vmem, vmem, vmem, hbm, hbm, vmem],
        out_specs=(vmem,) * 3,
        scratch_shapes=[
            pltpu.VMEM((length, 2 * width), jnp.bfloat16),
            pltpu.VMEM((2 * length, 2 * width), jnp.float32),
            pltpu.VMEM((2 * length, width), jnp.bfloat16),
            pltpu.VMEM((length, width), jnp.bfloat16),
            pltpu.VMEM((2 * length, length), jnp.bfloat16),
            pltpu.VMEM((length, 2 * length), jnp.bfloat16),
            dma((2,)),
            dma((outer - 1, 2)),
            dma((outer - 1, 2)),
            dma((outer - 1,)),
            dma((outer - 1,)),
            dma((groups - 1,)),
            dma((groups - 1,)),
            dma((groups - 1,)),
            dma((groups - 1,)),
        ],
        compiler_params=pltpu.CompilerParams(
            vmem_limit_bytes=60 * 1024 * 1024, collective_id=2, has_side_effects=True
        ),
        name="long_conv",
    )(
        key_feat,
        value_feat,
        long_filter,
        jnp.asarray(table.T, jnp.bfloat16),
        jnp.asarray(table, jnp.bfloat16),
        columns,
    )


def long_window(signal, kernel, outer):
    period = 2 * signal.shape[0]
    tokens = signal.shape[0] // outer
    stacked = jnp.stack([signal, kernel]).reshape(2, outer, tokens, -1).transpose(0, 3, 1, 2)
    real_part, imag_part = forward_outer(stacked, "scpm", 0, period)
    real_part, imag_part = forward_inner(real_part, imag_part, "sckm")
    real_part, imag_part = spectral_product(real_part, imag_part)
    real_part, imag_part = inverse_inner(real_part, imag_part, "ckm")
    local_mixed = inverse_outer(real_part, imag_part, "ckm", 0, period)
    return local_mixed.transpose(1, 2, 0).reshape(outer * tokens, -1)


def mix_blocks(tokens, outs, ins, chunk, real_ref, imag_ref, sum_ref, w_ref, spec_ref, row_of):
    for half in range(HALF // LANES):
        lanes = pl.ds(half * LANES, LANES)

        @pl.loop(0, outs // 2)
        def _(pair):
            def step(part, totals):
                totals = list(totals)
                for inner in range(chunk):
                    if inner % 8 == 0:
                        held = [
                            [
                                w_ref[
                                    pl.ds(pl.multiple_of(row_of(pair * 2 + b, part, inner), 8), 8),
                                    k * HALF + half * LANES : k * HALF + (half + 1) * LANES,
                                ]
                                for k in range(3)
                            ]
                            for b in range(2)
                        ]
                    rows = pl.ds(pl.multiple_of((part * chunk + inner) * tokens, tokens), tokens)
                    real = real_ref[rows, lanes]
                    imag = imag_ref[rows, lanes]
                    both = sum_ref[rows, lanes]
                    at = inner % 8
                    for b in range(2):
                        w0, w1, w2 = [held[b][k][at : at + 1] for k in range(3)]
                        totals[3 * b] = totals[3 * b] + w0 * both
                        totals[3 * b + 1] = totals[3 * b + 1] + w1 * real
                        totals[3 * b + 2] = totals[3 * b + 2] + w2 * imag
                return tuple(totals)

            zero = jnp.zeros((tokens, LANES), jnp.float32)
            totals = (zero,) * 6
            if ins == chunk:
                totals = step(0, totals)
            else:
                totals = lax.fori_loop(0, ins // chunk, step, totals)
            for b in range(2):
                rows = pl.ds(pl.multiple_of((pair * 2 + b) * tokens, tokens), tokens)
                cross, real, imag = totals[3 * b : 3 * b + 3]
                spec_ref[rows, half * LANES : (half + 1) * LANES] = (real - cross).astype(
                    jnp.bfloat16
                )
                spec_ref[rows, HALF + half * LANES : HALF + (half + 1) * LANES] = (
                    cross + imag
                ).astype(jnp.bfloat16)


def mlp_kernel(
    local,
    mine_ref,
    cols_ref,
    fwd_ref,
    inv_ref,
    tap_ref,
    out_ref,
    x_ref,
    done_ref,
    w_ref,
    rows_ref,
    hid_ref,
    spec_ref,
    real_ref,
    imag_ref,
    sum_ref,
    send_sem,
    recv_sem,
    back_send_sem,
    back_recv_sem,
):
    groups, tokens, width = mine_ref.shape
    per_group = width // BLOCK
    ins = groups * per_group
    tiles = groups * local
    stride = 2 * local * ins
    held = cols_ref.shape[0] // groups
    me = lax.axis_index("tp")
    peers = [lax.rem(me + d, groups) for d in range(1, groups)]

    barrier = pltpu.get_barrier_semaphore()
    for peer in peers:
        pl.semaphore_signal(
            barrier, inc=1, device_id={"tp": peer}, device_id_type=pl.DeviceIdType.MESH
        )
    pl.semaphore_wait(barrier, groups - 1)

    def send(d, src, dst, sent, got):
        copy = pltpu.make_async_remote_copy(
            src_ref=src.at[peers[d]],
            dst_ref=dst.at[me],
            send_sem=sent.at[d],
            recv_sem=got.at[d],
            device_id={"tp": peers[d]},
            device_id_type=pl.DeviceIdType.MESH,
        )
        copy.start()
        return copy

    copies = [send(d, mine_ref, x_ref, send_sem, recv_sem) for d in range(groups - 1)]
    x_ref[me] = mine_ref[me]
    for p in range(groups):
        for part in range(2):
            at = part * local * ins
            w_ref[p * stride + at : p * stride + at + local * ins, :] = jnp.dot(
                cols_ref[p * held + at : p * held + at + local * ins, :],
                tap_ref[...],
                preferred_element_type=jnp.float32,
            )
    for copy in copies:
        copy.wait()

    squares = jnp.zeros((tokens, 1), jnp.float32)
    for p in range(groups):
        wide = x_ref[p].astype(jnp.float32)
        squares = squares + jnp.sum(wide * wide, axis=1, keepdims=True)
    scale = lax.rsqrt(squares / (groups * width) + 1e-06)
    for j in range(ins):
        p, at = j // per_group, (j % per_group) * BLOCK
        wide = x_ref[p, :, at : at + BLOCK].astype(jnp.float32)
        row = p * held + stride + j % per_group
        gain = cols_ref[row : row + 1, :].astype(jnp.float32)
        rows_ref[j * tokens : (j + 1) * tokens, :] = (wide * scale * gain).astype(jnp.bfloat16)

    piece = 256

    def forward(values_ref, total):
        @pl.loop(0, total // piece)
        def _(at):
            rows = pl.ds(pl.multiple_of(at * piece, piece), piece)
            spec = jnp.dot(values_ref[rows, :], fwd_ref[...], preferred_element_type=jnp.float32)
            real_ref[rows, :] = spec[:, :HALF]
            imag_ref[rows, :] = spec[:, HALF:]
            sum_ref[rows, :] = spec[:, :HALF] + spec[:, HALF:]

    forward(rows_ref, ins * tokens)

    def up_row(i, part, inner):
        return (i // local) * stride + (i % local) * ins + inner

    mix_blocks(tokens, tiles, ins, ins, real_ref, imag_ref, sum_ref, w_ref, spec_ref, up_row)

    @pl.loop(0, tiles * tokens // piece)
    def _(at):
        rows = pl.ds(pl.multiple_of(at * piece, piece), piece)
        pre = jnp.dot(spec_ref[rows, :], inv_ref[...], preferred_element_type=jnp.float32)
        hidden = 0.5 * pre * (1.0 + lax.erf(pre * math.sqrt(0.5)))
        hid_ref[rows, :] = hidden.astype(jnp.bfloat16)

    forward(hid_ref, tiles * tokens)

    copies = []
    for d in range(groups):
        target = peers[d] if d < groups - 1 else me

        def down_row(i, part, inner):
            return part * stride + local * ins + (target * per_group + i) * local + inner

        mix_blocks(
            tokens, per_group, tiles, local, real_ref, imag_ref, sum_ref, w_ref, spec_ref, down_row
        )
        branch = jnp.dot(
            spec_ref[: per_group * tokens, :], inv_ref[...], preferred_element_type=jnp.float32
        )
        for i in range(per_group):
            at = i * BLOCK
            wide = x_ref[target, :, at : at + BLOCK].astype(jnp.float32)
            total = (wide + branch[i * tokens : (i + 1) * tokens]).astype(jnp.bfloat16)
            if d < groups - 1:
                done_ref[target, :, at : at + BLOCK] = total
            else:
                out_ref[target, :, at : at + BLOCK] = total
        if d < groups - 1:
            copies.append(send(d, done_ref, out_ref, back_send_sem, back_recv_sem))
    for copy in copies:
        copy.wait()


def mlp(stream, columns, local, forward_table, inverse_table, tap_table):
    groups, tokens, width = stream.shape
    ins = groups * width // BLOCK
    total = groups * local * tokens
    wide = pltpu.VMEM((total, HALF), jnp.float32)
    arrivals = pltpu.SemaphoreType.DMA((groups - 1,))
    return pl.pallas_call(
        functools.partial(mlp_kernel, local),
        out_shape=jax.ShapeDtypeStruct(stream.shape, jnp.bfloat16),
        in_specs=[pl.BlockSpec(memory_space=pltpu.VMEM)] * 5,
        out_specs=pl.BlockSpec(memory_space=pltpu.VMEM),
        scratch_shapes=[
            pltpu.VMEM(stream.shape, jnp.bfloat16),
            pltpu.VMEM(stream.shape, jnp.bfloat16),
            pltpu.VMEM((2 * groups * local * ins, 3 * HALF), jnp.float32),
            pltpu.VMEM((ins * tokens, BLOCK), jnp.bfloat16),
            pltpu.VMEM((total, BLOCK), jnp.bfloat16),
            pltpu.VMEM((total, BLOCK), jnp.bfloat16),
            wide,
            wide,
            wide,
            arrivals,
            arrivals,
            arrivals,
            arrivals,
        ],
        compiler_params=pltpu.CompilerParams(
            vmem_limit_bytes=40 * 1024 * 1024, collective_id=1, has_side_effects=True
        ),
        name="circulant_mlp",
    )(stream, columns, forward_table, inverse_table, tap_table)


def body(
    token_ids,
    embed_table,
    query_feat,
    key_feat,
    value_feat,
    long_filter,
    skip_gain,
    norm_gain,
    circulant_up,
    circulant_down,
):
    tokens = token_ids.shape[0]
    vocab = embed_table.shape[0]
    outer = lax.axis_size("ctx")
    groups = lax.axis_size("tp")
    width = query_feat.shape[1]
    ins = circulant_up.shape[1]
    local = circulant_up.shape[0]
    forward_table, inverse_table, tap_table = block_tables()
    gain_rows = norm_gain.reshape(-1, BLOCK)
    padded = 32
    gain_rows = jnp.pad(gain_rows, ((0, padded - gain_rows.shape[0]), (0, 0)))
    columns = jnp.concatenate(
        [circulant_up.reshape(-1, BLOCK), circulant_down.reshape(-1, BLOCK), gain_rows], axis=0
    )
    onehot = (token_ids[:, None] == lax.broadcasted_iota(jnp.int32, (1, vocab), 1)).astype(
        jnp.bfloat16
    )
    embedded = jnp.dot(onehot, embed_table, preferred_element_type=jnp.float32)
    if 2 * outer * tokens <= DENSE_WINDOW and width // outer % LANES == 0:
        mixed, gated, all_columns = short_window(
            key_feat, value_feat, long_filter, columns, outer, groups
        )
        all_columns = all_columns.reshape(-1, BLOCK)
        mixed = mixed.astype(jnp.float32)
    else:
        gated_wide = key_feat.astype(jnp.float32) * value_feat.astype(jnp.float32)
        gated = gated_wide.astype(jnp.bfloat16)
        pairs = jnp.concatenate(
            [gated.reshape(tokens, outer, -1), long_filter.reshape(tokens, outer, -1)], axis=2
        )
        arrived = lax.all_to_all(pairs, "ctx", split_axis=1, concat_axis=0)
        arrived = arrived.reshape(outer * tokens, -1)
        all_columns = lax.all_gather(columns, "tp", axis=0, tiled=True)
        local_mixed = long_window(*jnp.split(arrived, 2, axis=1), outer)
        mixed = lax.all_to_all(
            local_mixed.astype(jnp.bfloat16), "ctx", split_axis=0, concat_axis=1, tiled=True
        ).astype(jnp.float32)
    mixed = mixed + skip_gain[None, :] * gated.astype(jnp.float32)
    stream = (embedded + query_feat.astype(jnp.float32) * mixed).astype(jnp.bfloat16)
    own = stream.reshape(groups, tokens // groups, width)
    result = mlp(own, all_columns, local, forward_table, inverse_table, tap_table)
    return result.reshape(tokens, width)


def solution(mesh):
    placed = (
        P("ctx"),
        P(None, "tp"),
        P("ctx", "tp"),
        P("ctx", "tp"),
        P("ctx", "tp"),
        P("ctx", "tp"),
        P("tp"),
        P("tp"),
        P("tp", None, None),
        P(None, "tp", None),
    )
    return jax.shard_map(
        body, mesh=mesh, in_specs=placed, out_specs=P("ctx", "tp"), check_vma=False
    )
```
